256 devices in a mesh: gx: 32 (over y, z_lo, x), gy: 8 (over z_hi, core).
Axes of the slice: x: 4, y: 4, z: 8 (z_hi: 4, z_lo: 2; z = z_hi * 2 + z_lo), core: 2. Of those that a mesh axis runs over, the one named last changes fastest.
Arguments:
- features: bfloat16 [32, 8, 2, 512, 128], P('gx', 'gy'), may hold values from -6 to 6
- cotangent: bfloat16 [32, 8, 2, 512, 128], P('gx', 'gy'), may hold values from -6 to 6
- neighbours: int32 [32, 8, 2, 27], P('gx', 'gy'), may hold values from -1 to 17, as said below
- weights: bfloat16 [27, 128, 128], replicated, may hold values from -0.109375 to 0.109375
- channel_gain: float32 [128], replicated, may hold values from 0.5 to 2
Outputs:
- output: bfloat16 [32, 8, 2, 512, 128], P('gx', 'gy')
- input_grad: bfloat16 [32, 8, 2, 512, 128], P('gx', 'gy')
- weight_grad: float32 [27, 128, 128], replicated
- gain_grad: float32 [128], replicated
The draws below stay inside these ranges and needn't reach their ends.
Inputs may be any that keep to these rules, and one draw needn't show every extreme that they name: `neighbours`: entry [i, j, s, k] names, for slot s of device (i, j) and direction k = 9 (a + 1) + 3 (b + 1) + (c + 1), the block at block offset (a, b, c): the code (3 (i2 - i + 1) + (j2 - j + 1)) * 2 + s2 for slot s2 of device (i2, j2), always equal or beside (i, j), with i2 - i equal to 0 or a and j2 - j equal to 0 or b, or -1 where no occupied block lies. Codes are therefore at most 17. Entry 13 is 8 + s for an occupied slot; an empty slot has -1 everywhere. The relation is symmetric: the block named in direction k names the first one back in direction 26 - k. Some device has all 2 slots occupied.
All inputs are finite; a program needn't handle non-finite values.
Results may differ from the reference program's by a relative error of at most 0.0042.
Values may be sent and summed in bfloat16 or wider, within the bound.
No kernel may reach another device: no remote copies, remote signals or barrier semaphores. Data moves between devices by JAX's collectives and lax.ppermute only.
A program may use at most 64 MiB of HBM per device.

```python
import math
import jax
import jax.numpy as jnp
from jax import lax

C = 128
VOXELS = 512
CAP = 2
GRID_X = 32
GRID_Y = 8


def draw_neighbours(key, part):
    positions = 4 * CAP
    devices = GRID_X * GRID_Y
    base = jax.random.fold_in(key, 7)
    order_key, count_key, full_key = jax.random.split(base, 3)
    device_keys = jax.random.split(order_key, devices)
    position_order = jax.vmap(lambda single: jax.random.permutation(single, positions))(device_keys).astype(jnp.int32)
    occupied_count = jax.random.randint(count_key, (devices,), max(1, CAP // 4), CAP + 1).astype(jnp.int32)
    full_device = jax.random.randint(full_key, (), 0, devices).astype(jnp.int32)
    device_ids = jnp.arange(devices, dtype=jnp.int32)
    occupied_count = jnp.where(device_ids == full_device, CAP, occupied_count)
    ranking = jnp.argsort(position_order, axis=1).astype(jnp.int32)
    slot_of_position = jnp.where(ranking < occupied_count[:, None], ranking, -1)
    world_slots = slot_of_position.reshape(GRID_X, GRID_Y, 2, 2, CAP).transpose(0, 2, 1, 3, 4)
    world_slots = world_slots.reshape(2 * GRID_X, 2 * GRID_Y, CAP)
    world_slots = jnp.pad(world_slots, 1, constant_values=-1)
    chosen = position_order[:, :CAP]
    slot_ids = jnp.arange(CAP, dtype=jnp.int32)
    present = slot_ids[None, :] < occupied_count[:, None]
    pos_x = chosen // (2 * CAP)
    pos_y = chosen // CAP % 2
    pos_z = chosen % CAP
    row_index = (device_ids // GRID_Y)[:, None]
    col_index = (device_ids % GRID_Y)[:, None]
    world_x = 2 * row_index + pos_x
    world_y = 2 * col_index + pos_y
    offsets = jnp.array([(a, b, c) for a in (-1, 0, 1) for b in (-1, 0, 1) for c in (-1, 0, 1)], dtype=jnp.int32)
    step_x = offsets[:, 0][None, None, :]
    step_y = offsets[:, 1][None, None, :]
    step_z = offsets[:, 2][None, None, :]
    target_x = world_x[:, :, None] + step_x
    target_y = world_y[:, :, None] + step_y
    target_z = pos_z[:, :, None] + step_z
    found = world_slots[target_x + 1, target_y + 1, target_z + 1]
    owner_x = jnp.floor_divide(target_x, 2)
    owner_y = jnp.floor_divide(target_y, 2)
    direction = (owner_x - row_index[:, :, None] + 1) * 3 + (owner_y - col_index[:, :, None] + 1)
    code_value = direction * CAP + found
    code_value = jnp.where((found >= 0) & present[:, :, None], code_value, -1)
    return code_value.reshape(GRID_X, GRID_Y, CAP, 27).astype(jnp.int32)


def steps_of(stream_key, extent, shards, least, high):
    gain = 1.0
    for position, blocks in shards:
        heights = jax.random.uniform(jax.random.fold_in(jax.random.fold_in(stream_key, 6), position), (blocks,), jnp.float32, least / len(shards), high / len(shards))
        gain = gain * jnp.repeat(jnp.exp(heights), extent[position] // blocks).reshape((-1,) + (1,) * (len(extent) - 1 - position))
    return gain


def scatter_about(rng, dims, width, most, cuts=(), kind=jnp.bfloat16):
    loudness = steps_of(rng, dims, cuts, -0.22, 0.18) if cuts else 1.0
    values = jax.random.normal(rng, dims, jnp.float32) * width * loudness
    return jnp.minimum(jnp.maximum(values, -most), most).astype(kind)


def setup_inputs(seed: int = 0) -> dict:
    arg_keys = jax.random.split(jax.random.key(seed), 6)
    features = scatter_about(arg_keys[0], (GRID_X, GRID_Y, CAP, VOXELS, C), 1.0, 6.0, ((0, 32), (1, 8)))
    cotangent = scatter_about(arg_keys[1], (GRID_X, GRID_Y, CAP, VOXELS, C), 1.0, 6.0, ((0, 32), (1, 8)))
    neighbours = draw_neighbours(jax.random.fold_in(arg_keys[5], 71), 0)
    weights = scatter_about(arg_keys[3], (27, C, C), (27 * C) ** -0.5, 0.109375)
    channel_gain = jnp.clip(jnp.exp(jax.random.uniform(arg_keys[4], (C,), jnp.float32, math.log(0.5), math.log(2.0))), 0.5, 2.0)
    return dict(features=features, cotangent=cotangent, neighbours=neighbours, weights=weights, channel_gain=channel_gain)


DIRECTIONS = [(a, b, c) for a in (-1, 0, 1) for b in (-1, 0, 1) for c in (-1, 0, 1)]


def rim_range(d):
    if d < 0:
        return slice(7, 8)
    if d == 0:
        return slice(0, 8)
    return slice(0, 1)


def assemble(own_blocks, gathered_table, slot_codes):
    planes = []
    for a in (-1, 0, 1):
        row_parts = []
        for b in (-1, 0, 1):
            col_parts = []
            for c in (-1, 0, 1):
                k = (a + 1) * 9 + (b + 1) * 3 + (c + 1)
                if k == 13:
                    block_piece = own_blocks
                else:
                    region = gathered_table[:, rim_range(a), rim_range(b), rim_range(c)]
                    block_piece = jnp.take(region, jnp.maximum(slot_codes[:, k], 0), axis=0)
                    present = (slot_codes[:, k] >= 0)[:, None, None, None, None]
                    block_piece = jnp.where(present, block_piece, jnp.zeros((), block_piece.dtype))
                col_parts.append(block_piece)
            row_parts.append(jnp.concatenate(col_parts, axis=3))
        planes.append(jnp.concatenate(row_parts, axis=2))
    return jnp.concatenate(planes, axis=1)


def window(padded_tile, a, b, c):
    capacity = padded_tile.shape[0]
    channels = padded_tile.shape[-1]
    return padded_tile[:, 1 + a:9 + a, 1 + b:9 + b, 1 + c:9 + c].reshape(capacity * 512, channels)


def convolve(padded_tile, weights):
    total = None
    for k in range(27):
        a, b, c = DIRECTIONS[k]
        term = jnp.dot(window(padded_tile, a, b, c), weights[k], preferred_element_type=jnp.float32)
        total = term if total is None else total + term
    return total


def convolve_adjoint(padded_tile, weights):
    total = None
    for k in range(27):
        a, b, c = DIRECTIONS[k]
        term = jnp.dot(window(padded_tile, -a, -b, -c), weights[k].T, preferred_element_type=jnp.float32)
        total = term if total is None else total + term
    return total


def weight_terms(padded_tile, scaled):
    terms = []
    for k in range(27):
        a, b, c = DIRECTIONS[k]
        terms.append(jnp.dot(window(padded_tile, a, b, c).T, scaled, preferred_element_type=jnp.float32))
    return jnp.stack(terms, axis=0)


def reference(features, cotangent, neighbours, weights, channel_gain):
    capacity = features.shape[2]
    channels = features.shape[-1]
    occupied = (neighbours[:, :, :, 13] >= 0)[..., None, None]
    masked_x = jnp.where(occupied, features, jnp.zeros((), features.dtype))
    masked_dy = jnp.where(occupied, cotangent, jnp.zeros((), cotangent.dtype))
    pad_spec = ((1, 1), (1, 1), (0, 0), (0, 0), (0, 0))
    features_pad = jnp.pad(masked_x, pad_spec)
    device_ids = jnp.arange(GRID_X * GRID_Y, dtype=jnp.int32)

    def neighbourhood(padded, device_id):
        row_index = (device_id // GRID_Y).astype(jnp.int32)
        col_index = (device_id % GRID_Y).astype(jnp.int32)
        zero_index = jnp.zeros((), jnp.int32)
        region = lax.dynamic_slice(padded, (row_index, col_index, zero_index, zero_index, zero_index),
                                   (3, 3, capacity, 512, channels))
        gathered_table = region.reshape(9 * capacity, 8, 8, 8, channels)
        own_blocks = region[1, 1].reshape(capacity, 8, 8, 8, channels)
        return gathered_table, own_blocks, row_index, col_index

    def forward_device(device_id):
        gathered_table, own_blocks, row_index, col_index = neighbourhood(features_pad, device_id)
        slot_codes = neighbours[row_index, col_index]
        tile_x = assemble(own_blocks, gathered_table, slot_codes)
        conv_out = convolve(tile_x, weights)
        pre_act = own_blocks.reshape(-1, channels).astype(jnp.float32) + channel_gain * conv_out
        sigmoid_value = jax.nn.sigmoid(pre_act)
        result = (pre_act * sigmoid_value).astype(jnp.bfloat16)
        upstream = masked_dy[row_index, col_index].reshape(-1, channels).astype(jnp.float32)
        pre_grad = upstream * sigmoid_value * (1.0 + pre_act * (1.0 - sigmoid_value))
        scaled = (channel_gain * pre_grad).astype(jnp.bfloat16)
        gain_part = jnp.sum(pre_grad * conv_out, axis=0)
        return result, pre_grad, scaled, gain_part

    results, pre_grads, scaled_all, gain_parts = lax.map(forward_device, device_ids)
    scaled_pad = jnp.pad(scaled_all.reshape(GRID_X, GRID_Y, capacity, 512, channels), pad_spec)

    def backward_device(carry, device_id):
        table_x, own_x, row_index, col_index = neighbourhood(features_pad, device_id)
        table_u, own_u, row_again, col_again = neighbourhood(scaled_pad, device_id)
        slot_codes = neighbours[row_index, col_index]
        tile_x = assemble(own_x, table_x, slot_codes)
        tile_u = assemble(own_u, table_u, slot_codes)
        grad_here = (pre_grads[device_id] + convolve_adjoint(tile_u, weights)).astype(jnp.bfloat16)
        carry = carry + weight_terms(tile_x, own_u.reshape(-1, channels))
        return carry, grad_here

    weight_grad, input_grads = lax.scan(backward_device, jnp.zeros((27, channels, channels), jnp.float32), device_ids)
    output = results.reshape(GRID_X, GRID_Y, capacity, 512, channels)
    input_grad = input_grads.reshape(GRID_X, GRID_Y, capacity, 512, channels)
    gain_grad = jnp.sum(gain_parts, axis=0)
    return (output, input_grad, weight_grad, gain_grad)
```

```python
import jax
import jax.numpy as jnp
from jax import lax
from jax.experimental import pallas as pl
from jax.experimental.pallas import tpu as pltpu
from jax.sharding import PartitionSpec as P

C = 128
CAP = 2
SIDE = (-1, 0, 1)
EMPTY = 9 * CAP
VMEM = pltpu.VMEM
f32 = jnp.float32
bf16 = jnp.bfloat16


def rim(d):
    return {-1: (7, 1), 0: (0, 8), 1: (0, 1)}[d]


def place(d):
    return {-1: (0, 1), 0: (1, 8), 1: (9, 1)}[d]


def write_rims(value, out):
    x_low, x_high, y_low, y_high, edge_ll, edge_lh, edge_hl, edge_hh = out
    for ref, x in ((x_low, 0), (x_high, 7)):
        ref[...] = value[:, x].reshape(CAP * 64, C).astype(bf16)
    for ref, y in ((y_low, 0), (y_high, 7)):
        ref[...] = value[:, :, y].reshape(CAP * 64, C).astype(bf16)
    for ref, x, y in ((edge_ll, 0, 0), (edge_lh, 0, 7), (edge_hl, 7, 0), (edge_hh, 7, 7)):
        ref[...] = value[:, x, y].reshape(CAP * 8, C).astype(bf16)


def rim_shapes():
    return [jax.ShapeDtypeStruct((CAP * 64, C), bf16)] * 4 + [jax.ShapeDtypeStruct((CAP * 8, C), bf16)] * 4


def rims_kernel(x_ref, *out):
    write_rims(x_ref[...].astype(f32).reshape(CAP, 8, 8, 8, C), out)


def rims_of(x):
    return pl.pallas_call(
        rims_kernel,
        out_shape=rim_shapes(),
        in_specs=[pl.BlockSpec(memory_space=VMEM)],
        out_specs=[pl.BlockSpec(memory_space=VMEM)] * 8,
    )(x)


def exchange(rims):
    x_low, x_high, y_low, y_high, edge_ll, edge_lh, edge_hl, edge_hh = rims
    nx, ny = lax.axis_size("gx"), lax.axis_size("gy")

    def shift(value, dx, dy):
        pairs = []
        for i in range(nx):
            for j in range(ny):
                if 0 <= i + dx < nx and 0 <= j + dy < ny:
                    pairs.append((i * ny + j, (i + dx) * ny + j + dy))
        return lax.ppermute(value, ("gx", "gy"), pairs)

    return (
        shift(x_high, 1, 0),
        shift(x_low, -1, 0),
        shift(y_high, 0, 1),
        shift(y_low, 0, -1),
        shift(edge_hh, 1, 1),
        shift(edge_hl, 1, -1),
        shift(edge_lh, -1, 1),
        shift(edge_ll, -1, -1),
    )


def fill_table(table, own, halo):
    from_xm, from_xp, from_ym, from_yp, from_mm, from_mp, from_pm, from_pp = halo
    table[4 * CAP : 5 * CAP] = own.astype(f32).reshape(CAP, 8, 64, C)
    table[EMPTY] = jnp.zeros((8, 64, C), f32)
    for ref, device, x in ((from_xm, 1, 7), (from_xp, 7, 0)):
        table[device * CAP : (device + 1) * CAP, x] = ref[...].astype(f32).reshape(CAP, 64, C)
    for ref, device, y in ((from_ym, 3, 7), (from_yp, 5, 0)):
        table[device * CAP : (device + 1) * CAP, :, 8 * y : 8 * y + 8] = ref[...].astype(f32).reshape(CAP, 8, 8, C)
    for ref, device, x, y in ((from_mm, 0, 7, 7), (from_mp, 2, 7, 0), (from_pm, 6, 0, 7), (from_pp, 8, 0, 0)):
        table[device * CAP : (device + 1) * CAP, x, 8 * y : 8 * y + 8] = ref[...].astype(f32).reshape(CAP, 8, C)


def unfold(codes, table, planes, unfolded):
    height = lax.broadcasted_iota(jnp.int32, (1, 8, C), 1)
    for s in range(CAP):
        for a in SIDE:
            for b in SIDE:
                (xs, nx), (ys, ny) = rim(a), rim(b)
                (xd, _), (yd, _) = place(a), place(b)
                parts = []
                for c in SIDE:
                    code = codes[s, 9 * (a + 1) + 3 * (b + 1) + (c + 1)]
                    code = jnp.where(code < 0, EMPTY, code)
                    part = table[code, xs : xs + nx, 8 * ys : 8 * (ys + ny), :]
                    parts.append(part.reshape(nx * ny, 8, C))
                below, here, above = parts
                down = pltpu.roll(jnp.where(height == 7, below, here), 1, 1)
                up = pltpu.roll(jnp.where(height == 0, above, here), 7, 1)
                for i, part in enumerate((down, here, up)):
                    planes[i, xd : xd + nx, 8 * yd : 8 * (yd + ny), :] = part.reshape(nx, ny * 8, C)
        for b in SIDE:
            for c in SIDE:
                at = C * (3 * (b + 1) + (c + 1))
                unfolded[s, :, :, at : at + C] = planes[c + 1, :, 8 * (1 + b) : 8 * (1 + b) + 64, :].astype(bf16)


def forward_kernel(codes, x_ref, dy_ref, w_ref, gain_ref, *refs):
    halo, refs = refs[:8], refs[8:]
    out_ref, pre_grad_ref, scaled_ref, terms_ref = refs[:4]
    rim_refs, refs = refs[4:12], refs[12:]
    table, planes, unfolded, shifted = refs
    fill_table(table, x_ref[...], halo)
    unfold(codes, table, planes, unfolded)
    gain = gain_ref[...]
    gain_sum = jnp.zeros((1, C), f32)
    rim_values = []
    for s in range(CAP):
        conv = jnp.zeros((512, C), f32)
        for a in range(3):
            conv = conv + jnp.dot(
                unfolded[s, a : a + 8].reshape(512, 9 * C), w_ref[a], preferred_element_type=f32
            )
        occupied = codes[s, 13] >= 0
        own = jnp.where(occupied, x_ref[s].astype(f32), 0.0)
        upstream = jnp.where(occupied, dy_ref[s].astype(f32), 0.0)
        pre_act = own + gain * conv
        sig = jax.nn.sigmoid(pre_act)
        out_ref[s] = (pre_act * sig).astype(bf16)
        pre_grad = upstream * sig * (1.0 + pre_act * (1.0 - sig))
        pre_grad_ref[s] = pre_grad
        scaled = (gain * pre_grad).astype(bf16)
        scaled_ref[s] = scaled
        rim_values.append(scaled.astype(f32).reshape(1, 8, 8, 8, C))
        gain_sum = gain_sum + jnp.sum(pre_grad * conv, axis=0, keepdims=True)
        for a in range(3):
            at = C * a
            shifted[s, a : a + 8, :, at : at + C] = scaled.reshape(8, 64, C)
            for x in range(10):
                if not a <= x < a + 8:
                    shifted[s, x, :, at : at + C] = jnp.zeros((64, C), bf16)
    write_rims(jnp.concatenate(rim_values, axis=0), rim_refs)
    rhs = shifted[...].reshape(CAP * 640, 3 * C)
    for bc in range(9):
        lhs = unfolded[:, :, :, C * bc : C * bc + C].reshape(CAP * 640, C)
        term = lax.dot_general(lhs, rhs, (((0,), (0,)), ((), ())), preferred_element_type=f32)
        for a in range(3):
            terms_ref[9 * a + bc] = term[:, C * a : C * a + C]
    terms_ref[27] = jnp.concatenate([gain_sum, jnp.zeros((C - 1, C), f32)], axis=0)


def forward(codes, x, dy, weights, gain, halo):
    block = jax.ShapeDtypeStruct((CAP, 512, C), bf16)
    vmem = pl.BlockSpec(memory_space=VMEM)
    return pl.pallas_call(
        forward_kernel,
        out_shape=[
            block,
            jax.ShapeDtypeStruct((CAP, 512, C), f32),
            block,
            jax.ShapeDtypeStruct((28, C, C), f32),
            *rim_shapes(),
        ],
        in_specs=[pl.BlockSpec(memory_space=pltpu.SMEM)] + [vmem] * 12,
        out_specs=[vmem] * 12,
        scratch_shapes=[
            VMEM((EMPTY + 1, 8, 64, C), f32),
            VMEM((3, 10, 80, C), f32),
            VMEM((CAP, 10, 64, 9 * C), bf16),
            VMEM((CAP, 10, 64, 3 * C), bf16),
        ],
        compiler_params=pltpu.CompilerParams(vmem_limit_bytes=40 * 2**20),
    )(codes, x, dy, weights, gain, *halo)


def backward_kernel(codes, scaled_ref, w_ref, pre_grad_ref, *refs):
    halo, (grad_ref, table, planes, unfolded) = refs[:8], refs[8:]
    fill_table(table, scaled_ref[...], halo)
    unfold(codes, table, planes, unfolded)
    for s in range(CAP):
        total = pre_grad_ref[s]
        for a in range(3):
            total = total + jnp.dot(
                unfolded[s, a : a + 8].reshape(512, 9 * C), w_ref[a], preferred_element_type=f32
            )
        grad_ref[s] = total.astype(bf16)


def backward(codes, scaled, weights, pre_grad, halo):
    vmem = pl.BlockSpec(memory_space=VMEM)
    return pl.pallas_call(
        backward_kernel,
        out_shape=jax.ShapeDtypeStruct((CAP, 512, C), bf16),
        in_specs=[pl.BlockSpec(memory_space=pltpu.SMEM)] + [vmem] * 11,
        out_specs=vmem,
        scratch_shapes=[
            VMEM((EMPTY + 1, 8, 64, C), f32),
            VMEM((3, 10, 80, C), f32),
            VMEM((CAP, 10, 64, 9 * C), bf16),
        ],
        compiler_params=pltpu.CompilerParams(vmem_limit_bytes=40 * 2**20),
    )(codes, scaled, weights, pre_grad, *halo)


def on_device(features, cotangent, neighbours, weights, channel_gain):
    codes = neighbours[0, 0]
    x = features[0, 0]
    dy = cotangent[0, 0]
    halo = exchange(rims_of(x))
    result, pre_grad, scaled, terms, *rims = forward(
        codes, x, dy, weights.reshape(3, 9 * C, C), channel_gain.reshape(1, C), halo
    )
    adjoint = jnp.swapaxes(weights[::-1], 1, 2).reshape(3, 9 * C, C)
    grad = backward(codes, scaled, adjoint, pre_grad, exchange(rims))
    total = lax.psum(terms, ("gx", "gy"))
    return (result[None, None], grad[None, None], total[:27], total[27, 0])


def solution(mesh):
    split = P("gx", "gy", None, None, None)
    return jax.shard_map(
        on_device,
        mesh=mesh,
        in_specs=(split, split, P("gx", "gy", None, None), P(), P()),
        out_specs=(split, split, P(), P()),
        check_vma=False,
    )
```

```python
import jax
import jax.numpy as jnp
from jax import lax
from jax.experimental import pallas as pl
from jax.experimental.pallas import tpu as pltpu
from jax.sharding import Mesh, PartitionSpec as P

C = 128
CAP = 2
SIDE = (-1, 0, 1)
EMPTY = 9 * CAP
HALF = 14
GAIN_ROW = 16
SPLIT = (4, 2, 4, 4, 2)
AXES = ("y", "zl", "x", "zh", "core")
VMEM = pltpu.VMEM
f32 = jnp.float32
bf16 = jnp.bfloat16


def rim(d):
    return {-1: (7, 1), 0: (0, 8), 1: (0, 1)}[d]


def place(d):
    return {-1: (0, 1), 0: (1, 8), 1: (9, 1)}[d]


def write_rims(value, out):
    x_low, x_high, y_low, y_high = out
    for ref, x in ((x_low, 0), (x_high, 7)):
        ref[...] = value[:, x].reshape(CAP * 64, C).astype(bf16)
    for ref, y in ((y_low, 0), (y_high, 7)):
        ref[...] = value[:, :, y].reshape(CAP * 64, C).astype(bf16)


RIMS = [jax.ShapeDtypeStruct((CAP * 64, C), bf16)] * 4


def load_kernel(x_hbm, dy_hbm, w_hbm, x_ref, dy_ref, w_ref, *refs):
    out, sems = refs[:4], refs[4]
    copies = [
        pltpu.make_async_copy(src, dst, sems.at[i])
        for i, (src, dst) in enumerate(((x_hbm, x_ref), (dy_hbm, dy_ref), (w_hbm, w_ref)))
    ]
    for copy in copies:
        copy.start()
    copies[0].wait()
    write_rims(x_ref[...].astype(f32).reshape(CAP, 8, 8, 8, C), out)
    copies[1].wait()
    copies[2].wait()


def load(x, dy, weights):
    here = [jax.ShapeDtypeStruct(v.shape, v.dtype) for v in (x, dy, weights)]
    return pl.pallas_call(
        load_kernel,
        out_shape=[*here, *RIMS],
        in_specs=[pl.BlockSpec(memory_space=pltpu.HBM)] * 3,
        out_specs=[pl.BlockSpec(memory_space=VMEM)] * 7,
        scratch_shapes=[pltpu.SemaphoreType.DMA((3,))],
        compiler_params=pltpu.CompilerParams(vmem_limit_bytes=16 * 2**20),
    )(x, dy, weights)


def adjoint_kernel(w_ref, out_ref):
    for k in range(27):
        at = C * (k % 9)
        out_ref[k // 9, at : at + C] = w_ref[26 - k].astype(f32).T.astype(bf16)


def adjoint_of(weights):
    return pl.pallas_call(
        adjoint_kernel,
        out_shape=jax.ShapeDtypeStruct((3, 9 * C, C), bf16),
        in_specs=[pl.BlockSpec(memory_space=VMEM)],
        out_specs=pl.BlockSpec(memory_space=VMEM),
        compiler_params=pltpu.CompilerParams(vmem_limit_bytes=8 * 2**20),
    )(weights)


def widen_kernel(before_ref, after_ref, low_ref, high_ref, low_out, high_out):
    before = before_ref[...].astype(f32).reshape(CAP, 1, 8, 8, C)
    after = after_ref[...].astype(f32).reshape(CAP, 1, 8, 8, C)
    for y, own, out in ((0, low_ref, low_out), (7, high_ref, high_out)):
        middle = own[...].astype(f32).reshape(CAP, 8, 8, C)
        wide = jnp.concatenate([before[:, :, y], middle, after[:, :, y]], axis=1)
        out[...] = wide.reshape(CAP * 80, C).astype(bf16)


def widen(before, after, low, high):
    return pl.pallas_call(
        widen_kernel,
        out_shape=[jax.ShapeDtypeStruct((CAP * 80, C), bf16)] * 2,
        in_specs=[pl.BlockSpec(memory_space=VMEM)] * 4,
        out_specs=[pl.BlockSpec(memory_space=VMEM)] * 2,
        compiler_params=pltpu.CompilerParams(vmem_limit_bytes=4 * 2**20),
    )(before, after, low, high)


def shift(value, dx, dy):
    ny = lax.axis_size("zh") * lax.axis_size("core")
    nx = lax.axis_size(AXES) // ny
    pairs = []
    for i in range(nx):
        for j in range(ny):
            if 0 <= i + dx < nx and 0 <= j + dy < ny:
                pairs.append((i * ny + j, (i + dx) * ny + j + dy))
    return lax.ppermute(value, AXES, pairs)


def fill_table(table, own, halo):
    from_xm, from_xp, from_ym, from_yp = halo
    table[4 * CAP : 5 * CAP] = own.astype(f32).reshape(CAP, 8, 64, C)
    table[EMPTY] = jnp.zeros((8, 64, C), f32)
    for ref, device, x in ((from_xm, 1, 7), (from_xp, 7, 0)):
        table[device * CAP : (device + 1) * CAP, x] = ref[...].astype(f32).reshape(CAP, 64, C)
    for ref, dy, y in ((from_ym, 0, 7), (from_yp, 2, 0)):
        wide = ref[...].astype(f32).reshape(CAP, 10, 8, C)
        for dx, at, x, count in ((0, 0, 7, 1), (1, 1, 0, 8), (2, 9, 0, 1)):
            device = 3 * dx + dy
            table[device * CAP : (device + 1) * CAP, x : x + count, 8 * y : 8 * y + 8] = wide[:, at : at + count]


def unfold(codes, table, planes, unfolded):
    height = lax.broadcasted_iota(jnp.int32, (1, 8, C), 1)
    for s in range(CAP):
        for a in SIDE:
            for b in SIDE:
                (xs, nx), (ys, ny) = rim(a), rim(b)
                (xd, _), (yd, _) = place(a), place(b)
                parts = []
                for c in SIDE:
                    code = codes[s, 9 * (a + 1) + 3 * (b + 1) + (c + 1)]
                    code = jnp.where(code < 0, EMPTY, code)
                    part = table[code, xs : xs + nx, 8 * ys : 8 * (ys + ny), :]
                    parts.append(part.reshape(nx * ny, 8, C))
                below, here, above = parts
                down = pltpu.roll(jnp.where(height == 7, below, here), 1, 1)
                up = pltpu.roll(jnp.where(height == 0, above, here), 7, 1)
                for i, part in enumerate((down, here, up)):
                    planes[i, xd : xd + nx, 8 * yd : 8 * (yd + ny), :] = part.reshape(nx, ny * 8, C)
        for b in SIDE:
            for c in SIDE:
                at = C * (3 * (b + 1) + (c + 1))
                unfolded[s, :, :, at : at + C] = planes[c + 1, :, 8 * (1 + b) : 8 * (1 + b) + 64, :].astype(bf16)


def split_gain(rows, at, here):
    total = rows[at : at + 8] + rows[at + 8 : at + 16]
    high = total.astype(bf16).astype(f32)
    pair = jnp.concatenate([high, total - high], axis=0)
    pair = jnp.where(here, pair, rows[at : at + 16])
    pieces = [rows[:at]] if at else []
    return jnp.concatenate([*pieces, pair, rows[at + 16 :]], axis=0)


def forward_kernel(codes, core, x_ref, dy_ref, w_ref, gain_ref, *refs):
    halo, refs = refs[:4], refs[4:]
    out_ref, pre_grad_ref, scaled_ref, keep_ref, send_ref = refs[:5]
    rim_refs, refs = refs[5:9], refs[9:]
    table, planes, unfolded, shifted, terms = refs
    fill_table(table, x_ref[...], halo)
    unfold(codes, table, planes, unfolded)
    gain = gain_ref[...]
    gain_sum = jnp.zeros((1, C), f32)
    rim_values = []
    for s in range(CAP):
        conv = jnp.zeros((512, C), f32)
        for a in range(3):
            conv = conv + jnp.dot(
                unfolded[s, a : a + 8].reshape(512, 9 * C), w_ref[a], preferred_element_type=f32
            )
        occupied = codes[s, 13] >= 0
        own = jnp.where(occupied, x_ref[s].astype(f32), 0.0)
        upstream = jnp.where(occupied, dy_ref[s].astype(f32), 0.0)
        pre_act = own + gain * conv
        sig = jax.nn.sigmoid(pre_act)
        out_ref[s] = (pre_act * sig).astype(bf16)
        pre_grad = upstream * sig * (1.0 + pre_act * (1.0 - sig))
        pre_grad_ref[s] = pre_grad
        scaled = (gain * pre_grad).astype(bf16)
        scaled_ref[s] = scaled
        rim_values.append(scaled.astype(f32).reshape(1, 8, 8, 8, C))
        gain_sum = gain_sum + jnp.sum(pre_grad * conv, axis=0, keepdims=True)
        for a in range(3):
            at = C * a
            shifted[s, a : a + 8, :, at : at + C] = scaled.reshape(8, 64, C)
            for x in range(10):
                if not a <= x < a + 8:
                    shifted[s, x, :, at : at + C] = jnp.zeros((64, C), bf16)
    write_rims(jnp.concatenate(rim_values, axis=0), rim_refs)
    rhs = shifted[...].reshape(CAP * 640, 3 * C)
    for bc in range(9):
        lhs = unfolded[:, :, :, C * bc : C * bc + C].reshape(CAP * 640, C)
        term = lax.dot_general(lhs, rhs, (((0,), (0,)), ((), ())), preferred_element_type=f32)
        for a in range(3):
            half, block = divmod(9 * a + bc, HALF)
            terms[half, block] = term[:, C * a : C * a + C]
    first = jnp.concatenate([gain_sum, jnp.zeros((7, C), f32)], axis=0)
    high = first.astype(bf16).astype(f32)
    terms[1, HALF - 1] = jnp.zeros((C, C), f32)
    terms[1, HALF - 1, GAIN_ROW : GAIN_ROW + 16] = jnp.concatenate([high, first - high], axis=0)
    keep_ref[...] = terms[core[0]].reshape(HALF * C, C)
    send_ref[...] = terms[1 - core[0]].reshape(HALF * C, C).astype(bf16)


def forward(codes, core, x, dy, weights, gain, halo):
    block = jax.ShapeDtypeStruct((CAP, 512, C), bf16)
    vmem = pl.BlockSpec(memory_space=VMEM)
    smem = pl.BlockSpec(memory_space=pltpu.SMEM)
    return pl.pallas_call(
        forward_kernel,
        out_shape=[
            block,
            jax.ShapeDtypeStruct((CAP, 512, C), f32),
            block,
            jax.ShapeDtypeStruct((HALF * C, C), f32),
            jax.ShapeDtypeStruct((HALF * C, C), bf16),
            *RIMS,
        ],
        in_specs=[smem] * 2 + [vmem] * 8,
        out_specs=[vmem] * 9,
        scratch_shapes=[
            VMEM((EMPTY + 1, 8, 64, C), f32),
            VMEM((3, 10, 80, C), f32),
            VMEM((CAP, 10, 64, 9 * C), bf16),
            VMEM((CAP, 10, 64, 3 * C), bf16),
            VMEM((2, HALF, C, C), f32),
        ],
        compiler_params=pltpu.CompilerParams(vmem_limit_bytes=40 * 2**20),
    )(codes, core, x, dy, weights, gain, *halo)


def backward_kernel(codes, scaled_ref, w_ref, pre_grad_ref, *refs):
    halo, (grad_ref, table, planes, unfolded) = refs[:4], refs[4:]
    fill_table(table, scaled_ref[...], halo)
    unfold(codes, table, planes, unfolded)
    for s in range(CAP):
        total = pre_grad_ref[s]
        for a in range(3):
            total = total + jnp.dot(
                unfolded[s, a : a + 8].reshape(512, 9 * C), w_ref[a], preferred_element_type=f32
            )
        grad_ref[s] = total.astype(bf16)


def backward(codes, scaled, weights, pre_grad, halo):
    vmem = pl.BlockSpec(memory_space=VMEM)
    return pl.pallas_call(
        backward_kernel,
        out_shape=jax.ShapeDtypeStruct((CAP, 512, C), bf16),
        in_specs=[pl.BlockSpec(memory_space=pltpu.SMEM)] + [vmem] * 7,
        out_specs=vmem,
        scratch_shapes=[
            VMEM((EMPTY + 1, 8, 64, C), f32),
            VMEM((3, 10, 80, C), f32),
            VMEM((CAP, 10, 64, 9 * C), bf16),
        ],
        compiler_params=pltpu.CompilerParams(vmem_limit_bytes=40 * 2**20),
    )(codes, scaled, weights, pre_grad, *halo)


def pair_kernel(core, keep_ref, arrived_ref, out_ref):
    total = keep_ref[...] + arrived_ref[...].astype(f32)
    total = split_gain(total, (HALF - 1) * C + GAIN_ROW, core[0] == 1)
    out_ref[...] = total.astype(bf16).reshape(out_ref.shape)


def sum_kernel(last, parts_ref, out_ref):
    total = jnp.sum(parts_ref[...].astype(f32), axis=0)
    rows = total.shape[0]
    total = split_gain(total, rows - C + GAIN_ROW, last[0] == 1)
    out_ref[...] = jnp.broadcast_to(total.astype(bf16)[None], out_ref.shape)


def finish_kernel(core, mine_ref, other_ref, weight_ref, gain_ref):
    mine = mine_ref[...].reshape(HALF * C, C).astype(f32)
    other = other_ref[...].reshape(HALF * C, C).astype(f32)
    first = core[0] == 0
    weight_ref[:HALF] = jnp.where(first, mine, other).reshape(HALF, C, C)
    second = jnp.where(first, other, mine)
    weight_ref[HALF:] = second[: (HALF - 1) * C].reshape(HALF - 1, C, C)
    at = (HALF - 1) * C + GAIN_ROW
    gain_ref[...] = second[at : at + 8] + second[at + 8 : at + 16]


def small(kernel, out_shape, scalar, *operands):
    vmem = pl.BlockSpec(memory_space=VMEM)
    return pl.pallas_call(
        kernel,
        out_shape=out_shape,
        in_specs=[pl.BlockSpec(memory_space=pltpu.SMEM)] + [vmem] * len(operands),
        out_specs=jax.tree.map(lambda _: vmem, out_shape),
        compiler_params=pltpu.CompilerParams(vmem_limit_bytes=40 * 2**20),
    )(scalar, *operands)


def trade(parts, axes):
    return lax.all_to_all(parts, axes, 0, 0, tiled=True)


def on_device(features, cotangent, neighbours, weights, channel_gain):
    together = lax.optimization_barrier
    plane, line = ("y", "x"), ("zl", "zh")
    n_plane, n_line = lax.axis_size(plane), lax.axis_size(line)
    rows = HALF * C // n_plane
    swap = [(0, 1), (1, 0)]
    core = lax.axis_index("core").astype(jnp.int32).reshape(1)
    last = core * (lax.axis_index(plane) == n_plane - 1).astype(jnp.int32)
    codes = neighbours[0, 0]

    x, dy, weights, x_low, x_high, y_low, y_high = load(features[0, 0], cotangent[0, 0], weights)
    before, after, adjoint = together((shift(x_high, 1, 0), shift(x_low, -1, 0), adjoint_of(weights)))
    low, high = widen(before, after, y_low, y_high)
    halo = (before, after, shift(high, 0, 1), shift(low, 0, -1))
    result, pre_grad, scaled, keep, send, x_low, x_high, y_low, y_high = forward(
        codes, core, x, dy, weights.reshape(3, 9 * C, C), channel_gain.reshape(1, C), halo
    )

    before, after, arrived = together(
        (shift(x_high, 1, 0), shift(x_low, -1, 0), lax.ppermute(send, "core", swap))
    )
    low, high = widen(before, after, y_low, y_high)
    parts = small(pair_kernel, jax.ShapeDtypeStruct((n_plane, rows, C), bf16), core, keep, arrived)
    below, above, parts = together((shift(high, 0, 1), shift(low, 0, -1), trade(parts, plane)))
    grad = backward(codes, scaled, adjoint, pre_grad, (before, after, below, above))
    parts = small(sum_kernel, jax.ShapeDtypeStruct((n_line, rows, C), bf16), last, parts)
    parts = small(sum_kernel, jax.ShapeDtypeStruct((n_plane, rows, C), bf16), last, trade(parts, line))
    mine = trade(parts, plane)
    other = lax.ppermute(mine, "core", swap)
    shapes = (jax.ShapeDtypeStruct((27, C, C), f32), jax.ShapeDtypeStruct((8, C), f32))
    weight_grad, gain_grad = small(finish_kernel, shapes, core, mine, other)
    return (result[None, None], grad[None, None], weight_grad, gain_grad[0])


def solution(mesh):
    physical = Mesh(mesh.devices.reshape(SPLIT), AXES)
    gx, gy = ("y", "zl", "x"), ("zh", "core")
    split = P(gx, gy, None, None, None)
    return jax.shard_map(
        on_device,
        mesh=physical,
        in_specs=(split, split, P(gx, gy, None, None), P(), P()),
        out_specs=(split, split, P(), P()),
        check_vma=False,
    )
```

```python
import jax
import jax.numpy as jnp
from jax import lax
from jax.experimental import pallas as pl
from jax.experimental.pallas import tpu as pltpu
from jax.sharding import Mesh, PartitionSpec as P

C = 128
CAP = 2
SIDE = (-1, 0, 1)
EMPTY = 9 * CAP
HALF = 14
GAIN_ROW = 16
CORE, ODD, LAST = 0, 1, 2
SPLIT = (4, 2, 4, 4, 2)
AXES = ("y", "zl", "x", "zh", "core")
VMEM = pltpu.VMEM
f32 = jnp.float32
bf16 = jnp.bfloat16
BLOCK = jax.ShapeDtypeStruct((CAP, 512, C), bf16)


def rim(d):
    return {-1: (7, 1), 0: (0, 8), 1: (0, 1)}[d]


def place(d):
    return {-1: (0, 1), 0: (1, 8), 1: (9, 1)}[d]


def y_planes(value):
    value = value.astype(f32).reshape(CAP, 8, 8, 8, C)
    return [value[:, :, y].reshape(CAP * 64, C) for y in (0, 7)]


def rims_kernel(place, x_ref, near_ref, far_ref, x_out):
    x_out[...] = x_ref[...]
    low, high = y_planes(x_ref[...])
    first = place[CORE] == 0
    near_ref[...] = jnp.where(first, high, low).astype(bf16)
    far_ref[...] = jnp.where(first, low, high).astype(bf16)


def rims_of(place, x):
    plane = jax.ShapeDtypeStruct((CAP * 64, C), bf16)
    return small(rims_kernel, [plane, plane, BLOCK], 8, place, x)


def adjoint_kernel(w_ref, out_ref):
    for k in range(27):
        at = C * (k % 9)
        out_ref[k // 9, at : at + C] = w_ref[26 - k].astype(f32).T.astype(bf16)


def adjoint_of(weights):
    return small(adjoint_kernel, jax.ShapeDtypeStruct((3, 9 * C, C), bf16), 8, None, weights)


def fetch_kernel(value_ref, out_ref):
    out_ref[...] = value_ref[...]


def fetch(value):
    return small(fetch_kernel, BLOCK, 8, None, value)


def widen_kernel(place, near_ref, far_ref, x_ref, first_ref, second_ref):
    before, after = sides(place[CORE] == 0, near_ref, far_ref)
    wide = []
    for x in (0, 7):
        middle = x_ref[:, 64 * x : 64 * x + 64].astype(f32).reshape(CAP, 8, 8, C)
        ends = [v.reshape(CAP, 8, 8, C)[:, x : x + 1] for v in (before, after)]
        wide.append(jnp.concatenate([ends[0], middle, ends[1]], axis=1).reshape(CAP * 80, C))
    even = place[ODD] == 0
    first_ref[...] = jnp.where(even, wide[1], wide[0]).astype(bf16)
    second_ref[...] = jnp.where(even, wide[0], wide[1]).astype(bf16)


def widen(place, near, far, x):
    shapes = [jax.ShapeDtypeStruct((CAP * 80, C), bf16)] * 2
    return small(widen_kernel, shapes, 8, place, near, far, x)


def sides(first, one_ref, other_ref):
    one, other = one_ref[...].astype(f32), other_ref[...].astype(f32)
    return jnp.where(first, other, one), jnp.where(first, one, other)


def swap_far(value):
    n = lax.axis_size("zh")
    pairs = [(2 * i + 1, 2 * i + 2) for i in range(n - 1)]
    return lax.ppermute(value, ("zh", "core"), pairs + [(b, a) for a, b in pairs])


def swap_x(value, odd):
    axes = ("y", "zl", "x")
    pairs = [(i, i + 1) for i in range(odd, lax.axis_size(axes) - 1, 2)]
    return lax.ppermute(value, axes, pairs + [(b, a) for a, b in pairs])


def swap_core(value):
    return lax.ppermute(value, "core", [(0, 1), (1, 0)])


def fill_table(place, table, own, halo):
    near, far, first, second = halo
    table[4 * CAP : 5 * CAP] = own.astype(f32).reshape(CAP, 8, 64, C)
    table[EMPTY] = jnp.zeros((8, 64, C), f32)
    for value, device, y in zip(sides(place[CORE] == 0, near, far), (3, 5), (7, 0)):
        table[device * CAP : (device + 1) * CAP, :, 8 * y : 8 * y + 8] = value.reshape(CAP, 8, 8, C)
    for value, dx, x in zip(sides(place[ODD] == 0, first, second), (0, 2), (7, 0)):
        wide = value.reshape(CAP, 80, C)
        for dy, at, y, count in ((0, 0, 7, 1), (1, 1, 0, 8), (2, 9, 0, 1)):
            device = 3 * dx + dy
            table[device * CAP : (device + 1) * CAP, x, 8 * y : 8 * (y + count)] = wide[:, 8 * at : 8 * (at + count)]


def unfold(codes, table, planes, unfolded):
    height = lax.broadcasted_iota(jnp.int32, (1, 8, C), 1)
    for s in range(CAP):
        for a in SIDE:
            for b in SIDE:
                (xs, nx), (ys, ny) = rim(a), rim(b)
                (xd, _), (yd, _) = place(a), place(b)
                parts = []
                for c in SIDE:
                    code = codes[s, 9 * (a + 1) + 3 * (b + 1) + (c + 1)]
                    code = jnp.where(code < 0, EMPTY, code)
                    part = table[code, xs : xs + nx, 8 * ys : 8 * (ys + ny), :]
                    parts.append(part.reshape(nx * ny, 8, C))
                below, here, above = parts
                down = pltpu.roll(jnp.where(height == 7, below, here), 1, 1)
                up = pltpu.roll(jnp.where(height == 0, above, here), 7, 1)
                for i, part in enumerate((down, here, up)):
                    planes[i, xd : xd + nx, 8 * yd : 8 * (yd + ny), :] = part.reshape(nx, ny * 8, C)
        for b in SIDE:
            for c in SIDE:
                at = C * (3 * (b + 1) + (c + 1))
                unfolded[s, :, :, at : at + C] = planes[c + 1, :, 8 * (1 + b) : 8 * (1 + b) + 64, :].astype(bf16)


def split_gain(rows, at, here):
    total = rows[at : at + 8] + rows[at + 8 : at + 16]
    high = total.astype(bf16).astype(f32)
    pair = jnp.concatenate([high, total - high], axis=0)
    pair = jnp.where(here, pair, rows[at : at + 16])
    pieces = [rows[:at]] if at else []
    return jnp.concatenate([*pieces, pair, rows[at + 16 :]], axis=0)


def forward_kernel(codes, place, x_ref, dy_ref, w_ref, gain_ref, *refs):
    halo, refs = refs[:4], refs[4:]
    out_ref, pre_grad_ref, scaled_ref, keep_ref, send_ref, far_ref = refs[:6]
    table, planes, unfolded, shifted, terms, staged, sems = refs[6:]
    fill_table(place, table, x_ref[...], halo)
    unfold(codes, table, planes, unfolded)
    gain = gain_ref[...]
    gain_sum = jnp.zeros((1, C), f32)
    for s in range(CAP):
        conv = jnp.zeros((512, C), f32)
        for a in range(3):
            conv = conv + jnp.dot(
                unfolded[s, a : a + 8].reshape(512, 9 * C), w_ref[a], preferred_element_type=f32
            )
        occupied = codes[s, 13] >= 0
        upstream = jnp.where(occupied, dy_ref[s].astype(f32), 0.0)
        pre_act = jnp.where(occupied, x_ref[s].astype(f32), 0.0) + gain * conv
        sig = jax.nn.sigmoid(pre_act)
        staged[s] = (pre_act * sig).astype(bf16)
        pltpu.make_async_copy(staged.at[s], out_ref.at[s], sems.at[s]).start()
        pre_grad = upstream * sig * (1.0 + pre_act * (1.0 - sig))
        pre_grad_ref[s] = pre_grad
        scaled = (gain * pre_grad).astype(bf16)
        scaled_ref[s] = scaled
        gain_sum = gain_sum + jnp.sum(pre_grad * conv, axis=0, keepdims=True)
        for a in range(3):
            at = C * a
            shifted[s, a : a + 8, :, at : at + C] = scaled.reshape(8, 64, C)
            for x in range(10):
                if not a <= x < a + 8:
                    shifted[s, x, :, at : at + C] = jnp.zeros((64, C), bf16)
    core = place[CORE]
    low, high = y_planes(scaled_ref[...])
    far_ref[...] = jnp.where(core == 0, low, high).astype(bf16)
    send_ref[HALF * C :] = jnp.where(core == 0, high, low).astype(bf16)
    rhs = shifted[...].reshape(CAP * 640, 3 * C)
    for bc in range(9):
        lhs = unfolded[:, :, :, C * bc : C * bc + C].reshape(CAP * 640, C)
        term = lax.dot_general(lhs, rhs, (((0,), (0,)), ((), ())), preferred_element_type=f32)
        for a in range(3):
            half, block = divmod(9 * a + bc, HALF)
            terms[half, block] = term[:, C * a : C * a + C]
    first = jnp.concatenate([gain_sum, jnp.zeros((7, C), f32)], axis=0)
    high = first.astype(bf16).astype(f32)
    terms[1, HALF - 1] = jnp.zeros((C, C), f32)
    terms[1, HALF - 1, GAIN_ROW : GAIN_ROW + 16] = jnp.concatenate([high, first - high], axis=0)
    keep_ref[...] = terms[core].reshape(HALF * C, C)
    send_ref[: HALF * C] = terms[1 - core].reshape(HALF * C, C).astype(bf16)
    for s in range(CAP):
        pltpu.make_async_copy(staged.at[s], out_ref.at[s], sems.at[s]).wait()


def forward(codes, place, x, dy, weights, gain, halo):
    vmem = pl.BlockSpec(memory_space=VMEM)
    smem = pl.BlockSpec(memory_space=pltpu.SMEM)
    return pl.pallas_call(
        forward_kernel,
        out_shape=[
            BLOCK,
            jax.ShapeDtypeStruct((CAP, 512, C), f32),
            BLOCK,
            jax.ShapeDtypeStruct((HALF * C, C), f32),
            jax.ShapeDtypeStruct((HALF * C + CAP * 64, C), bf16),
            jax.ShapeDtypeStruct((CAP * 64, C), bf16),
        ],
        in_specs=[smem] * 2 + [vmem] * 8,
        out_specs=[pl.BlockSpec(memory_space=pltpu.HBM)] + [vmem] * 5,
        scratch_shapes=[
            VMEM((EMPTY + 1, 8, 64, C), f32),
            VMEM((3, 10, 80, C), f32),
            VMEM((CAP, 10, 64, 9 * C), bf16),
            VMEM((CAP, 10, 64, 3 * C), bf16),
            VMEM((2, HALF, C, C), f32),
            VMEM((CAP, 512, C), bf16),
            pltpu.SemaphoreType.DMA((CAP,)),
        ],
        compiler_params=pltpu.CompilerParams(vmem_limit_bytes=40 * 2**20),
    )(codes, place, x, dy, weights, gain, *halo)


def backward_kernel(codes, place, scaled_ref, w_ref, pre_grad_ref, *refs):
    halo, (grad_ref, table, planes, unfolded, staged, sems) = refs[:4], refs[4:]
    fill_table(place, table, scaled_ref[...], halo)
    unfold(codes, table, planes, unfolded)
    for s in range(CAP):
        total = pre_grad_ref[s]
        for a in range(3):
            total = total + jnp.dot(
                unfolded[s, a : a + 8].reshape(512, 9 * C), w_ref[a], preferred_element_type=f32
            )
        staged[s] = total.astype(bf16)
        pltpu.make_async_copy(staged.at[s], grad_ref.at[s], sems.at[s]).start()
    for s in range(CAP):
        pltpu.make_async_copy(staged.at[s], grad_ref.at[s], sems.at[s]).wait()


def backward(codes, place, scaled, weights, pre_grad, halo):
    vmem = pl.BlockSpec(memory_space=VMEM)
    return pl.pallas_call(
        backward_kernel,
        out_shape=BLOCK,
        in_specs=[pl.BlockSpec(memory_space=pltpu.SMEM)] * 2 + [vmem] * 7,
        out_specs=pl.BlockSpec(memory_space=pltpu.HBM),
        scratch_shapes=[
            VMEM((EMPTY + 1, 8, 64, C), f32),
            VMEM((3, 10, 80, C), f32),
            VMEM((CAP, 10, 64, 9 * C), bf16),
            VMEM((CAP, 512, C), bf16),
            pltpu.SemaphoreType.DMA((CAP,)),
        ],
        compiler_params=pltpu.CompilerParams(vmem_limit_bytes=40 * 2**20),
    )(codes, place, scaled, weights, pre_grad, *halo)


def pair_kernel(place, keep_ref, arrived_ref, out_ref, near_ref):
    total = keep_ref[...] + arrived_ref[: HALF * C].astype(f32)
    total = split_gain(total, (HALF - 1) * C + GAIN_ROW, place[CORE] == 1)
    out_ref[...] = total.astype(bf16).reshape(out_ref.shape)
    near_ref[...] = arrived_ref[HALF * C :]


def sum_kernel(place, parts_ref, out_ref):
    total = jnp.sum(parts_ref[...].astype(f32), axis=0)
    rows = total.shape[0]
    total = split_gain(total, rows - C + GAIN_ROW, place[LAST] == 1)
    out_ref[...] = jnp.broadcast_to(total.astype(bf16)[None], out_ref.shape)


def write_half(second, rows_ref, weight_ref, staged, sem):
    staged[...] = rows_ref[...].reshape(HALF, C, C).astype(f32)

    @pl.when(second)
    def _():
        copy = pltpu.make_async_copy(staged.at[: HALF - 1], weight_ref.at[HALF:], sem)
        copy.start()
        copy.wait()

    @pl.when(jnp.logical_not(second))
    def _():
        copy = pltpu.make_async_copy(staged, weight_ref.at[:HALF], sem)
        copy.start()
        copy.wait()


def mine_kernel(place, mine_ref, weight_ref, staged, sem):
    write_half(place[CORE] == 1, mine_ref, weight_ref, staged, sem)


def other_kernel(place, mine_ref, other_ref, _, weight_ref, gain_hbm, staged, sem, gain_ref, gain_sem):
    at = (HALF - 1) * C + GAIN_ROW
    mine, other = (ref[...].reshape(HALF * C, C)[at : at + 16].astype(f32) for ref in (mine_ref, other_ref))
    pair = jnp.where(place[CORE] == 1, mine, other)
    gain_ref[...] = pair[:1] + pair[8:9]
    copy = pltpu.make_async_copy(gain_ref, gain_hbm, gain_sem)
    copy.start()
    write_half(place[CORE] == 0, other_ref, weight_ref, staged, sem)
    copy.wait()


def finish(place, mine, other):
    smem, vmem, hbm = (pl.BlockSpec(memory_space=m) for m in (pltpu.SMEM, VMEM, pltpu.HBM))
    weight_grad = jax.ShapeDtypeStruct((27, C, C), f32)
    scratch = [VMEM((HALF, C, C), f32), pltpu.SemaphoreType.DMA]
    params = pltpu.CompilerParams(vmem_limit_bytes=8 * 2**20)
    partial = pl.pallas_call(
        mine_kernel,
        out_shape=weight_grad,
        in_specs=[smem, vmem],
        out_specs=hbm,
        scratch_shapes=scratch,
        compiler_params=params,
    )(place, mine)
    return pl.pallas_call(
        other_kernel,
        out_shape=[weight_grad, jax.ShapeDtypeStruct((1, C), f32)],
        in_specs=[smem, vmem, vmem, hbm],
        out_specs=[hbm, hbm],
        scratch_shapes=[*scratch, VMEM((1, C), f32), pltpu.SemaphoreType.DMA],
        input_output_aliases={3: 0},
        compiler_params=params,
    )(place, mine, other, partial)


def small(kernel, out_shape, megabytes, scalars, *operands):
    vmem = pl.BlockSpec(memory_space=VMEM)
    smem = [] if scalars is None else [scalars]
    return pl.pallas_call(
        kernel,
        out_shape=out_shape,
        in_specs=[pl.BlockSpec(memory_space=pltpu.SMEM)] * len(smem) + [vmem] * len(operands),
        out_specs=jax.tree.map(lambda _: vmem, out_shape),
        compiler_params=pltpu.CompilerParams(vmem_limit_bytes=megabytes * 2**20),
    )(*smem, *operands)


def trade(parts, axes):
    return lax.all_to_all(parts, axes, 0, 0, tiled=True)


def on_device(features, cotangent, neighbours, weights, channel_gain):
    together = lax.optimization_barrier
    plane, line = ("y", "x"), ("zl", "zh")
    n_plane, n_line = lax.axis_size(plane), lax.axis_size(line)
    rows = HALF * C // n_plane
    core = lax.axis_index("core")
    last = core * (lax.axis_index(plane) == n_plane - 1)
    place = jnp.stack([core, lax.axis_index("x") % 2, last]).astype(jnp.int32)
    codes = neighbours[0, 0]
    near, far, x = rims_of(place, features[0, 0])
    near, far, adjoint = together((swap_core(near), swap_far(far), adjoint_of(weights)))
    first, second = widen(place, near, far, x)
    first, second, dy = together((swap_x(first, 0), swap_x(second, 1), fetch(cotangent[0, 0])))
    halo = (near, far, first, second)
    result, pre_grad, scaled, keep, send, far = forward(
        codes, place, x, dy, weights.reshape(3, 9 * C, C), channel_gain.reshape(1, C), halo
    )

    shapes = [jax.ShapeDtypeStruct((n_plane, rows, C), bf16), jax.ShapeDtypeStruct((CAP * 64, C), bf16)]
    parts, near = small(pair_kernel, shapes, 8, place, keep, swap_core(send))
    far, parts = together((swap_far(far), trade(parts, plane)))
    first, second = widen(place, near, far, scaled)
    parts = small(sum_kernel, jax.ShapeDtypeStruct((n_line, rows, C), bf16), 8, place, parts)
    first, second, parts = together((swap_x(first, 0), swap_x(second, 1), trade(parts, line)))
    parts = small(sum_kernel, jax.ShapeDtypeStruct((n_plane, rows, C), bf16), 8, place, parts)
    grad = backward(codes, place, scaled, adjoint, pre_grad, (near, far, first, second))
    grad, mine = together((grad, trade(parts, plane)))
    weight_grad, gain_grad = finish(place, mine, swap_core(mine))
    return (result[None, None], grad[None, None], weight_grad, gain_grad.reshape(C))


def solution(mesh):
    physical = Mesh(mesh.devices.reshape(SPLIT), AXES)
    gx, gy = ("y", "zl", "x"), ("zh", "core")
    split = P(gx, gy, None, None, None)
    return jax.shard_map(
        on_device,
        mesh=physical,
        in_specs=(split, split, P(gx, gy, None, None), P(), P()),
        out_specs=(split, split, P(), P()),
        check_vma=False,
    )
```

```python
import jax
import jax.numpy as jnp
from jax import lax
from jax.experimental import pallas as pl
from jax.experimental.pallas import tpu as pltpu
from jax.sharding import Mesh, PartitionSpec as P

C = 128
CAP = 2
SIDE = (-1, 0, 1)
EMPTY = 9 * CAP
HALF = 14
GAIN_ROW = 16
PIECES = 2
CORE, ODD, LAST = 0, 1, 2
SPLIT = (4, 2, 4, 4, 2)
AXES = ("y", "zl", "x", "zh", "core")
VMEM = pltpu.VMEM
f32 = jnp.float32
bf16 = jnp.bfloat16
BLOCK = jax.ShapeDtypeStruct((CAP, 512, C), bf16)


def rim(d):
    return {-1: (7, 1), 0: (0, 8), 1: (0, 1)}[d]


def span(d):
    return {-1: (0, 1), 0: (1, 8), 1: (9, 1)}[d]


def y_planes(value):
    value = value.astype(f32).reshape(CAP, 8, 8, 8, C)
    return [value[:, :, y].reshape(CAP * 64, C) for y in (0, 7)]


def rims_kernel(place, x_ref, near_ref, far_ref, x_out):
    x_out[...] = x_ref[...]
    low, high = y_planes(x_ref[...])
    first = place[CORE] == 0
    near_ref[...] = jnp.where(first, high, low).astype(bf16)
    far_ref[...] = jnp.where(first, low, high).astype(bf16)


def rims_of(place, x):
    plane = jax.ShapeDtypeStruct((CAP * 64, C), bf16)
    return small(rims_kernel, [plane, plane, BLOCK], 8, place, x)


def matrices_kernel(w_ref, adjoint_ref, ends_ref, adjoint_ends_ref):
    for k in range(27):
        a, at = k // 9, C * (k % 9)
        matrix = w_ref[26 - k].astype(f32).T.astype(bf16)
        adjoint_ref[a, at : at + C] = matrix
        if a != 1:
            column = 0 if a == 0 else C
            adjoint_ends_ref[at : at + C, column : column + C] = matrix
            ends_ref[at : at + C, column : column + C] = w_ref[k]


def matrices_of(weights):
    ends = jax.ShapeDtypeStruct((9 * C, 2 * C), bf16)
    shapes = [jax.ShapeDtypeStruct((3, 9 * C, C), bf16), ends, ends]
    return small(matrices_kernel, shapes, 8, None, weights)


def fetch_kernel(value_ref, out_ref):
    out_ref[...] = value_ref[...]


def fetch(value):
    return small(fetch_kernel, BLOCK, 8, None, value)


def widen_kernel(place, near_ref, far_ref, x_ref, first_ref, second_ref):
    before, after = sides(place[CORE] == 0, near_ref, far_ref)
    wide = []
    for x in (0, 7):
        middle = x_ref[:, 64 * x : 64 * x + 64].astype(f32).reshape(CAP, 8, 8, C)
        ends = [v.reshape(CAP, 8, 8, C)[:, x : x + 1] for v in (before, after)]
        wide.append(jnp.concatenate([ends[0], middle, ends[1]], axis=1).reshape(CAP * 80, C))
    even = place[ODD] == 0
    first_ref[...] = jnp.where(even, wide[1], wide[0]).astype(bf16)
    second_ref[...] = jnp.where(even, wide[0], wide[1]).astype(bf16)


def widen(place, near, far, x):
    shapes = [jax.ShapeDtypeStruct((CAP * 80, C), bf16)] * 2
    return small(widen_kernel, shapes, 8, place, near, far, x)


def sides(first, one_ref, other_ref):
    one, other = one_ref[...].astype(f32), other_ref[...].astype(f32)
    return jnp.where(first, other, one), jnp.where(first, one, other)


def swap_far(value):
    n = lax.axis_size("zh")
    pairs = [(2 * i + 1, 2 * i + 2) for i in range(n - 1)]
    return lax.ppermute(value, ("zh", "core"), pairs + [(b, a) for a, b in pairs])


def swap_x(value, odd):
    axes = ("y", "zl", "x")
    pairs = [(i, i + 1) for i in range(odd, lax.axis_size(axes) - 1, 2)]
    return lax.ppermute(value, axes, pairs + [(b, a) for a, b in pairs])


def swap_core(value):
    return lax.ppermute(value, "core", [(0, 1), (1, 0)])


def fill_own(place, table, own, near, far):
    table[4 * CAP : 5 * CAP] = own.astype(f32).reshape(CAP, 8, 64, C)
    table[EMPTY] = jnp.zeros((8, 64, C), f32)
    for value, device, y in zip(sides(place[CORE] == 0, near, far), (3, 5), (7, 0)):
        table[device * CAP : (device + 1) * CAP, :, 8 * y : 8 * y + 8] = value.reshape(CAP, 8, 8, C)


def fill_table(place, table, own, halo):
    near, far, first, second = halo
    fill_own(place, table, own, near, far)
    for value, dx, x in zip(sides(place[ODD] == 0, first, second), (0, 2), (7, 0)):
        wide = value.reshape(CAP, 80, C)
        for dy, at, y, count in ((0, 0, 7, 1), (1, 1, 0, 8), (2, 9, 0, 1)):
            device = 3 * dx + dy
            table[device * CAP : (device + 1) * CAP, x, 8 * y : 8 * (y + count)] = wide[:, 8 * at : 8 * (at + count)]


ALL = {-1: 0, 0: 1, 1: 9}
MIDDLE = {0: 0}
RIM = {-1: 0, 1: 1}


def unfold(codes, table, planes, unfolded, places):
    height = lax.broadcasted_iota(jnp.int32, (1, 8, C), 1)
    for s in range(CAP):
        for a, xd in places.items():
            for b in SIDE:
                (xs, nx), (ys, ny) = rim(a), rim(b)
                yd, _ = span(b)
                parts = []
                for c in SIDE:
                    code = codes[s, 9 * (a + 1) + 3 * (b + 1) + (c + 1)]
                    code = jnp.where(code < 0, EMPTY, code)
                    part = table[code, xs : xs + nx, 8 * ys : 8 * (ys + ny), :]
                    parts.append(part.reshape(nx * ny, 8, C))
                below, here, above = parts
                down = pltpu.roll(jnp.where(height == 7, below, here), 1, 1)
                up = pltpu.roll(jnp.where(height == 0, above, here), 7, 1)
                for i, part in enumerate((down, here, up)):
                    planes[i, xd : xd + nx, 8 * yd : 8 * (yd + ny), :] = part.reshape(nx, ny * 8, C)
        for b in SIDE:
            for c in SIDE:
                at = C * (3 * (b + 1) + (c + 1))
                unfolded[s, :, :, at : at + C] = planes[c + 1, :, 8 * (1 + b) : 8 * (1 + b) + 64, :].astype(bf16)


def split_gain(rows, at, here):
    total = rows[at : at + 8] + rows[at + 8 : at + 16]
    high = total.astype(bf16).astype(f32)
    pair = jnp.concatenate([high, total - high], axis=0)
    pair = jnp.where(here, pair, rows[at : at + 16])
    pieces = [rows[:at]] if at else []
    return jnp.concatenate([*pieces, pair, rows[at + 16 :]], axis=0)


def middle_kernel(codes, place, x_ref, w_ref, ends_ref, near_ref, far_ref, conv_ref, middle_ref, table, planes):
    fill_own(place, table, x_ref[...], near_ref, far_ref)
    unfold(codes, table, planes, middle_ref, MIDDLE)
    for s in range(CAP):
        ends = dot_rows(middle_ref[s], ends_ref[...])
        conv_ref[s] = dot_rows(middle_ref[s], w_ref[1])
        conv_ref[s, 64:] += ends[:448, :C]
        conv_ref[s, :448] += ends[64:, C:]


def middle(codes, place, x, weights, ends, near, far, keep):
    vmem = pl.BlockSpec(memory_space=VMEM)
    smem = pl.BlockSpec(memory_space=pltpu.SMEM)
    conv = jax.ShapeDtypeStruct((CAP, 512, C), f32)
    scratch = [VMEM((EMPTY + 1, 8, 64, C), f32), VMEM((3, 8, 80, C), f32)]
    shape = (CAP, 8, 64, 9 * C)
    return pl.pallas_call(
        middle_kernel,
        out_shape=[conv, jax.ShapeDtypeStruct(shape, bf16)] if keep else [conv],
        in_specs=[smem] * 2 + [vmem] * 5,
        out_specs=[vmem] * (2 if keep else 1),
        scratch_shapes=scratch if keep else [VMEM(shape, bf16), *scratch],
        compiler_params=pltpu.CompilerParams(vmem_limit_bytes=24 * 2**20),
    )(codes, place, x, weights, ends, near, far)


def dot_rows(planes, matrix):
    rows = planes.shape[0] * planes.shape[1]
    return jnp.dot(planes.reshape(rows, planes.shape[2]), matrix, preferred_element_type=f32)


def forward_kernel(codes, place, x_ref, dy_ref, w_ref, gain_ref, conv_ref, middle_ref, *refs):
    halo, refs = refs[:4], refs[4:]
    out_ref, pre_grad_ref, scaled_ref, keep_ref, send_ref, far_ref = refs[:6]
    table, planes, rim_planes, conv_all, shifted, shifted_rim, terms, staged, sems = refs[6:]
    fill_table(place, table, x_ref[...], halo)
    unfold(codes, table, planes, rim_planes, RIM)
    conv_all[...] = conv_ref[...]
    conv_all[:, :64] += dot_rows(rim_planes[:, 0], w_ref[0]).reshape(CAP, 64, C)
    conv_all[:, 448:] += dot_rows(rim_planes[:, 1], w_ref[2]).reshape(CAP, 64, C)
    gain = gain_ref[...]
    gain_sum = jnp.zeros((1, C), f32)
    for s in range(CAP):
        conv = conv_all[s]
        occupied = codes[s, 13] >= 0
        upstream = jnp.where(occupied, dy_ref[s].astype(f32), 0.0)
        pre_act = jnp.where(occupied, x_ref[s].astype(f32), 0.0) + gain * conv
        sig = jax.nn.sigmoid(pre_act)
        staged[s] = (pre_act * sig).astype(bf16)
        pltpu.make_async_copy(staged.at[s], out_ref.at[s], sems.at[s]).start()
        pre_grad = upstream * sig * (1.0 + pre_act * (1.0 - sig))
        pre_grad_ref[s] = pre_grad
        scaled = (gain * pre_grad).astype(bf16)
        scaled_ref[s] = scaled
        gain_sum = gain_sum + jnp.sum(pre_grad * conv, axis=0, keepdims=True)
        scaled = scaled.reshape(8, 64, C)
        zero = jnp.zeros((64, C), bf16)
        shifted[s, :7, :, :C] = scaled[1:]
        shifted[s, 7, :, :C] = zero
        shifted[s, :, :, C : 2 * C] = scaled
        shifted[s, 0, :, 2 * C :] = zero
        shifted[s, 1:, :, 2 * C :] = scaled[:7]
        shifted_rim[s] = jnp.zeros((2, 64, 3 * C), bf16)
        shifted_rim[s, 0, :, :C] = scaled[0]
        shifted_rim[s, 1, :, 2 * C :] = scaled[7]
    core = place[CORE]
    low, high = y_planes(scaled_ref[...])
    far_ref[...] = jnp.where(core == 0, low, high).astype(bf16)
    send_ref[HALF * C :] = jnp.where(core == 0, high, low).astype(bf16)
    pairs = ((middle_ref, shifted, CAP * 512), (rim_planes, shifted_rim, CAP * 128))
    for bc in range(9):
        term = jnp.zeros((C, 3 * C), f32)
        for source, target, rows in pairs:
            lhs = source[:, :, :, C * bc : C * bc + C].reshape(rows, C)
            rhs = target[...].reshape(rows, 3 * C)
            term = term + lax.dot_general(lhs, rhs, (((0,), (0,)), ((), ())), preferred_element_type=f32)
        for a in range(3):
            half, block = divmod(9 * a + bc, HALF)
            terms[half, block] = term[:, C * a : C * a + C]
    first = jnp.concatenate([gain_sum, jnp.zeros((7, C), f32)], axis=0)
    high = first.astype(bf16).astype(f32)
    terms[1, HALF - 1] = jnp.zeros((C, C), f32)
    terms[1, HALF - 1, GAIN_ROW : GAIN_ROW + 16] = jnp.concatenate([high, first - high], axis=0)
    keep_ref[...] = terms[core].reshape(HALF * C, C)
    send_ref[: HALF * C] = terms[1 - core].reshape(HALF * C, C).astype(bf16)
    for s in range(CAP):
        pltpu.make_async_copy(staged.at[s], out_ref.at[s], sems.at[s]).wait()


def forward(codes, place, x, dy, weights, gain, conv, unfolded, halo):
    vmem = pl.BlockSpec(memory_space=VMEM)
    smem = pl.BlockSpec(memory_space=pltpu.SMEM)
    return pl.pallas_call(
        forward_kernel,
        out_shape=[
            BLOCK,
            jax.ShapeDtypeStruct((CAP, 512, C), f32),
            BLOCK,
            jax.ShapeDtypeStruct((HALF * C, C), f32),
            jax.ShapeDtypeStruct((HALF * C + CAP * 64, C), bf16),
            jax.ShapeDtypeStruct((CAP * 64, C), bf16),
        ],
        in_specs=[smem] * 2 + [vmem] * 10,
        out_specs=[pl.BlockSpec(memory_space=pltpu.HBM)] + [vmem] * 5,
        scratch_shapes=[
            VMEM((EMPTY + 1, 8, 64, C), f32),
            VMEM((3, 2, 80, C), f32),
            VMEM((CAP, 2, 64, 9 * C), bf16),
            VMEM((CAP, 512, C), f32),
            VMEM((CAP, 8, 64, 3 * C), bf16),
            VMEM((CAP, 2, 64, 3 * C), bf16),
            VMEM((2, HALF, C, C), f32),
            VMEM((CAP, 512, C), bf16),
            pltpu.SemaphoreType.DMA((CAP,)),
        ],
        compiler_params=pltpu.CompilerParams(vmem_limit_bytes=32 * 2**20),
    )(codes, place, x, dy, weights, gain, conv, unfolded, *halo)


def backward_kernel(codes, place, scaled_ref, w_ref, pre_grad_ref, conv_ref, *refs):
    halo, (grad_ref, table, planes, rim_planes, staged, total, sems) = refs[:4], refs[4:]
    fill_table(place, table, scaled_ref[...], halo)
    unfold(codes, table, planes, rim_planes, RIM)
    total[...] = pre_grad_ref[...] + conv_ref[...]
    total[:, :64] += dot_rows(rim_planes[:, 0], w_ref[0]).reshape(CAP, 64, C)
    total[:, 448:] += dot_rows(rim_planes[:, 1], w_ref[2]).reshape(CAP, 64, C)
    staged[...] = total[...].astype(bf16)
    copy = pltpu.make_async_copy(staged, grad_ref, sems)
    copy.start()
    copy.wait()


def backward(codes, place, scaled, weights, pre_grad, conv, halo):
    vmem = pl.BlockSpec(memory_space=VMEM)
    return pl.pallas_call(
        backward_kernel,
        out_shape=BLOCK,
        in_specs=[pl.BlockSpec(memory_space=pltpu.SMEM)] * 2 + [vmem] * 8,
        out_specs=pl.BlockSpec(memory_space=pltpu.HBM),
        scratch_shapes=[
            VMEM((EMPTY + 1, 8, 64, C), f32),
            VMEM((3, 2, 80, C), f32),
            VMEM((CAP, 2, 64, 9 * C), bf16),
            VMEM((CAP, 512, C), bf16),
            VMEM((CAP, 512, C), f32),
            pltpu.SemaphoreType.DMA,
        ],
        compiler_params=pltpu.CompilerParams(vmem_limit_bytes=32 * 2**20),
    )(codes, place, scaled, weights, pre_grad, conv, *halo)


def pair_kernel(place, keep_ref, arrived_ref, out_hbm, near_ref, staged, sems):
    near_ref[...] = arrived_ref[HALF * C :]
    chunks, rows, _ = staged.shape
    copies = []
    for i in range(0, chunks, chunks // PIECES):
        piece = slice(i, i + chunks // PIECES)
        flat = slice(i * rows, (i + chunks // PIECES) * rows)
        total = keep_ref[flat] + arrived_ref[flat].astype(f32)
        at = (HALF - 1) * C + GAIN_ROW - flat.start
        if flat.stop == HALF * C:
            total = split_gain(total, at, place[CORE] == 1)
        staged[piece] = total.astype(bf16).reshape(chunks // PIECES, rows, C)
        copies.append(pltpu.make_async_copy(staged.at[piece], out_hbm.at[piece], sems.at[len(copies)]))
        copies[-1].start()
    for copy in copies:
        copy.wait()


def pair_sum(place, keep, arrived, chunks):
    smem, vmem, hbm = (pl.BlockSpec(memory_space=m) for m in (pltpu.SMEM, VMEM, pltpu.HBM))
    shape = (chunks, HALF * C // chunks, C)
    return pl.pallas_call(
        pair_kernel,
        out_shape=[jax.ShapeDtypeStruct(shape, bf16), jax.ShapeDtypeStruct((CAP * 64, C), bf16)],
        in_specs=[smem, vmem, vmem],
        out_specs=[hbm, vmem],
        scratch_shapes=[VMEM(shape, bf16), pltpu.SemaphoreType.DMA((PIECES,))],
        compiler_params=pltpu.CompilerParams(vmem_limit_bytes=8 * 2**20),
    )(place, keep, arrived)


def sum_kernel(place, parts_ref, out_ref):
    total = jnp.sum(parts_ref[...].astype(f32), axis=0)
    total = split_gain(total, total.shape[0] - C + GAIN_ROW, place[LAST] == 1)
    out_ref[...] = jnp.broadcast_to(total.astype(bf16)[None], out_ref.shape)


def sum_of(place, parts, count):
    return small(sum_kernel, jax.ShapeDtypeStruct((count, *parts.shape[1:]), bf16), 8, place, parts)


def write_half(second, rows_ref, weight_ref, staged, sems):
    rows = rows_ref[...].reshape(HALF, C, C)

    def copies(at, stop, i):
        here = slice(at, min(stop, HALF - 1))
        behind = pltpu.make_async_copy(staged.at[here], weight_ref.at[HALF + at : HALF + here.stop], sems.at[i])
        return behind, pltpu.make_async_copy(staged.at[at:stop], weight_ref.at[at:stop], sems.at[i])

    pieces = [copies(0, 7, 0), copies(7, HALF, 1)]
    for i, (behind, ahead) in enumerate(pieces):
        staged[7 * i : 7 * i + 7] = rows[7 * i : 7 * i + 7].astype(f32)
        pl.when(second)(behind.start)
        pl.when(jnp.logical_not(second))(ahead.start)
    for behind, ahead in pieces:
        pl.when(second)(behind.wait)
        pl.when(jnp.logical_not(second))(ahead.wait)


def mine_kernel(place, mine_ref, weight_ref, staged, sems):
    write_half(place[CORE] == 1, mine_ref, weight_ref, staged, sems)


def other_kernel(place, mine_ref, other_ref, _, weight_ref, gain_hbm, staged, sems, gain_ref, gain_sem):
    at = (HALF - 1) * C + GAIN_ROW
    mine, other = (ref[...].reshape(HALF * C, C)[at : at + 16].astype(f32) for ref in (mine_ref, other_ref))
    pair = jnp.where(place[CORE] == 1, mine, other)
    gain_ref[...] = pair[:1] + pair[8:9]
    copy = pltpu.make_async_copy(gain_ref, gain_hbm, gain_sem)
    copy.start()
    write_half(place[CORE] == 0, other_ref, weight_ref, staged, sems)
    copy.wait()


def finish(place, mine, other):
    smem, vmem, hbm = (pl.BlockSpec(memory_space=m) for m in (pltpu.SMEM, VMEM, pltpu.HBM))
    weight_grad = jax.ShapeDtypeStruct((27, C, C), f32)
    scratch = [VMEM((HALF, C, C), f32), pltpu.SemaphoreType.DMA((2,))]
    params = pltpu.CompilerParams(vmem_limit_bytes=8 * 2**20)
    partial = pl.pallas_call(
        mine_kernel,
        out_shape=weight_grad,
        in_specs=[smem, vmem],
        out_specs=hbm,
        scratch_shapes=scratch,
        compiler_params=params,
    )(place, mine)
    return pl.pallas_call(
        other_kernel,
        out_shape=[weight_grad, jax.ShapeDtypeStruct((1, C), f32)],
        in_specs=[smem, vmem, vmem, hbm],
        out_specs=[hbm, hbm],
        scratch_shapes=[*scratch, VMEM((1, C), f32), pltpu.SemaphoreType.DMA],
        input_output_aliases={3: 0},
        compiler_params=params,
    )(place, mine, other, partial)


def small(kernel, out_shape, megabytes, scalars, *operands):
    vmem = pl.BlockSpec(memory_space=VMEM)
    smem = [] if scalars is None else [scalars]
    return pl.pallas_call(
        kernel,
        out_shape=out_shape,
        in_specs=[pl.BlockSpec(memory_space=pltpu.SMEM)] * len(smem) + [vmem] * len(operands),
        out_specs=jax.tree.map(lambda _: vmem, out_shape),
        compiler_params=pltpu.CompilerParams(vmem_limit_bytes=megabytes * 2**20),
    )(*smem, *operands)


def trade(parts, axes):
    return lax.all_to_all(parts, axes, 0, 0, tiled=True)


def on_device(features, cotangent, neighbours, weights, channel_gain):
    together = lax.optimization_barrier
    plane, line = ("y", "x"), ("zl", "zh")
    n_plane, n_line = lax.axis_size(plane), lax.axis_size(line)
    core = lax.axis_index("core")
    last = core * (lax.axis_index(plane) == n_plane - 1)
    place = jnp.stack([core, lax.axis_index("x") % 2, last]).astype(jnp.int32)
    codes = neighbours[0, 0]
    near, far, x = rims_of(place, features[0, 0])
    near, far, (adjoint, ends, adjoint_ends), dy = together(
        (swap_core(near), swap_far(far), matrices_of(weights), fetch(cotangent[0, 0]))
    )
    first, second = widen(place, near, far, x)
    matrices = weights.reshape(3, 9 * C, C)
    conv, unfolded = middle(codes, place, x, matrices, ends, near, far, True)
    first, second, conv, unfolded = together((swap_x(first, 0), swap_x(second, 1), conv, unfolded))
    halo = (near, far, first, second)
    result, pre_grad, scaled, keep, send, far = forward(
        codes, place, x, dy, matrices, channel_gain.reshape(1, C), conv, unfolded, halo
    )

    parts, near = pair_sum(place, keep, swap_core(send), n_plane)
    far, parts = together((swap_far(far), trade(parts, plane)))
    first, second = widen(place, near, far, scaled)
    parts = sum_of(place, parts, n_line)
    (conv,) = middle(codes, place, scaled, adjoint, adjoint_ends, near, far, False)
    first, conv, parts = together((swap_x(first, 0), conv, trade(parts, line)))
    parts = sum_of(place, parts, n_plane)
    second = swap_x(second, 1)
    grad = backward(codes, place, scaled, adjoint, pre_grad, conv, (near, far, first, second))
    grad, mine = together((grad, trade(parts, plane)))
    weight_grad, gain_grad = finish(place, mine, swap_core(mine))
    return (result[None, None], grad[None, None], weight_grad, gain_grad.reshape(C))


def solution(mesh):
    physical = Mesh(mesh.devices.reshape(SPLIT), AXES)
    gx, gy = ("y", "zl", "x"), ("zh", "core")
    split = P(gx, gy, None, None, None)
    return jax.shard_map(
        on_device,
        mesh=physical,
        in_specs=(split, split, P(gx, gy, None, None), P(), P()),
        out_specs=(split, split, P(), P()),
        check_vma=False,
    )
```

```python
import jax
import jax.numpy as jnp
from jax import lax
from jax.experimental import pallas as pl
from jax.experimental.pallas import tpu as pltpu
from jax.sharding import Mesh, PartitionSpec as P

C = 128
CAP = 2
SIDE = (-1, 0, 1)
EMPTY = 9 * CAP
HALF = 14
GAIN_ROW = 16
PIECES = 2
CORE, ODD, LAST = 0, 1, 2
SPLIT = (4, 2, 4, 4, 2)
AXES = ("y", "zl", "x", "zh", "core")
VMEM = pltpu.VMEM
f32 = jnp.float32
bf16 = jnp.bfloat16
BLOCK = jax.ShapeDtypeStruct((CAP, 512, C), bf16)


def rim(d):
    return {-1: (7, 1), 0: (0, 8), 1: (0, 1)}[d]


def span(d):
    return {-1: (0, 1), 0: (1, 8), 1: (9, 1)}[d]


def y_planes(value):
    value = value.astype(f32).reshape(CAP, 8, 8, 8, C)
    return [value[:, :, y].reshape(CAP * 64, C) for y in (0, 7)]


def rims_kernel(place, x_ref, near_ref, far_ref, x_out):
    x_out[...] = x_ref[...]
    low, high = y_planes(x_ref[...])
    first = place[CORE] == 0
    near_ref[...] = jnp.where(first, high, low).astype(bf16)
    far_ref[...] = jnp.where(first, low, high).astype(bf16)


def rims_of(place, x):
    plane = jax.ShapeDtypeStruct((CAP * 64, C), bf16)
    return small(rims_kernel, [plane, plane, BLOCK], 8, place, x)


def prepare_kernel(w_ref, codes_ref, w_out, codes_out, adjoint_ref, ends_ref, adjoint_ends_ref):
    codes_out[...] = codes_ref[...]
    for k in range(27):
        a, at = k // 9, C * (k % 9)
        w_out[a, at : at + C] = w_ref[k]
        matrix = w_ref[26 - k].astype(f32).T.astype(bf16)
        adjoint_ref[a, at : at + C] = matrix
        if a != 1:
            column = 0 if a == 0 else C
            adjoint_ends_ref[at : at + C, column : column + C] = matrix
            ends_ref[at : at + C, column : column + C] = w_ref[k]


def prepare(weights, codes):
    ends = jax.ShapeDtypeStruct((9 * C, 2 * C), bf16)
    matrices = jax.ShapeDtypeStruct((3, 9 * C, C), bf16)
    shapes = [matrices, jax.ShapeDtypeStruct(codes.shape, codes.dtype), matrices, ends, ends]
    return small(prepare_kernel, shapes, 8, None, weights, codes)


def fetch_kernel(value_ref, out_ref):
    out_ref[...] = value_ref[...]


def fetch(value):
    return small(fetch_kernel, BLOCK, 8, None, value)


def widen_kernel(place, near_ref, far_ref, x_ref, first_ref, second_ref):
    before, after = sides(place[CORE] == 0, near_ref, far_ref)
    wide = []
    for x in (0, 7):
        middle = x_ref[:, 64 * x : 64 * x + 64].astype(f32).reshape(CAP, 8, 8, C)
        ends = [v.reshape(CAP, 8, 8, C)[:, x : x + 1] for v in (before, after)]
        wide.append(jnp.concatenate([ends[0], middle, ends[1]], axis=1).reshape(CAP * 80, C))
    even = place[ODD] == 0
    first_ref[...] = jnp.where(even, wide[1], wide[0]).astype(bf16)
    second_ref[...] = jnp.where(even, wide[0], wide[1]).astype(bf16)


def widen(place, near, far, x):
    shapes = [jax.ShapeDtypeStruct((CAP * 80, C), bf16)] * 2
    return small(widen_kernel, shapes, 8, place, near, far, x)


def sides(first, one_ref, other_ref):
    one, other = one_ref[...].astype(f32), other_ref[...].astype(f32)
    return jnp.where(first, other, one), jnp.where(first, one, other)


def swap_far(value):
    n = lax.axis_size("zh")
    pairs = [(2 * i + 1, 2 * i + 2) for i in range(n - 1)]
    return lax.ppermute(value, ("zh", "core"), pairs + [(b, a) for a, b in pairs])


def swap_x(value, odd):
    axes = ("y", "zl", "x")
    pairs = [(i, i + 1) for i in range(odd, lax.axis_size(axes) - 1, 2)]
    return lax.ppermute(value, axes, pairs + [(b, a) for a, b in pairs])


def swap_core(value):
    return lax.ppermute(value, "core", [(0, 1), (1, 0)])


def fill_own(place, table, own, near, far, planes):
    own = own.astype(f32).reshape(CAP, 8, 64, C)
    for x in planes:
        table[4 * CAP : 5 * CAP, x] = own[:, x]
        table[EMPTY, x] = jnp.zeros((64, C), f32)
    for value, device, y in zip(sides(place[CORE] == 0, near, far), (3, 5), (7, 0)):
        table[device * CAP : (device + 1) * CAP, :, 8 * y : 8 * y + 8] = value.reshape(CAP, 8, 8, C)


def fill_table(place, table, own, halo):
    near, far, first, second = halo
    fill_own(place, table, own, near, far, (0, 7))
    for value, dx, x in zip(sides(place[ODD] == 0, first, second), (0, 2), (7, 0)):
        wide = value.reshape(CAP, 80, C)
        for dy, at, y, count in ((0, 0, 7, 1), (1, 1, 0, 8), (2, 9, 0, 1)):
            device = 3 * dx + dy
            table[device * CAP : (device + 1) * CAP, x, 8 * y : 8 * (y + count)] = wide[:, 8 * at : 8 * (at + count)]


ALL = {-1: 0, 0: 1, 1: 9}
MIDDLE = {0: 0}
RIM = {-1: 0, 1: 1}


def unfold(codes, table, planes, unfolded, places):
    height = lax.broadcasted_iota(jnp.int32, (1, 8, C), 1)
    for s in range(CAP):
        for a, xd in places.items():
            for b in SIDE:
                (xs, nx), (ys, ny) = rim(a), rim(b)
                yd, _ = span(b)
                parts = []
                for c in SIDE:
                    code = codes[s, 9 * (a + 1) + 3 * (b + 1) + (c + 1)]
                    code = jnp.where(code < 0, EMPTY, code)
                    part = table[code, xs : xs + nx, 8 * ys : 8 * (ys + ny), :]
                    parts.append(part.reshape(nx * ny, 8, C))
                below, here, above = parts
                down = pltpu.roll(jnp.where(height == 7, below, here), 1, 1)
                up = pltpu.roll(jnp.where(height == 0, above, here), 7, 1)
                for i, part in enumerate((down, here, up)):
                    planes[i, xd : xd + nx, 8 * yd : 8 * (yd + ny), :] = part.reshape(nx, ny * 8, C)
        for b in SIDE:
            for c in SIDE:
                at = C * (3 * (b + 1) + (c + 1))
                unfolded[s, :, :, at : at + C] = planes[c + 1, :, 8 * (1 + b) : 8 * (1 + b) + 64, :].astype(bf16)


def split_gain(rows, at, here):
    total = rows[at : at + 8] + rows[at + 8 : at + 16]
    high = total.astype(bf16).astype(f32)
    pair = jnp.concatenate([high, total - high], axis=0)
    pair = jnp.where(here, pair, rows[at : at + 16])
    pieces = [rows[:at]] if at else []
    return jnp.concatenate([*pieces, pair, rows[at + 16 :]], axis=0)


def middle_kernel(codes, place, x_ref, w_ref, ends_ref, near_ref, far_ref, conv_ref, middle_ref, table, planes):
    fill_own(place, table, x_ref[...], near_ref, far_ref, range(8))
    unfold(codes, table, planes, middle_ref, MIDDLE)
    for s in range(CAP):
        ends = dot_rows(middle_ref[s], ends_ref[...])
        conv_ref[s] = dot_rows(middle_ref[s], w_ref[1])
        conv_ref[s, 64:] += ends[:448, :C]
        conv_ref[s, :448] += ends[64:, C:]


def middle(codes, place, x, weights, ends, near, far, keep):
    vmem = pl.BlockSpec(memory_space=VMEM)
    smem = pl.BlockSpec(memory_space=pltpu.SMEM)
    conv = jax.ShapeDtypeStruct((CAP, 512, C), f32)
    scratch = [VMEM((EMPTY + 1, 8, 64, C), f32), VMEM((3, 8, 80, C), f32)]
    shape = (CAP, 8, 64, 9 * C)
    return pl.pallas_call(
        middle_kernel,
        out_shape=[conv, jax.ShapeDtypeStruct(shape, bf16)] if keep else [conv],
        in_specs=[smem] * 2 + [vmem] * 5,
        out_specs=[vmem] * (2 if keep else 1),
        scratch_shapes=scratch if keep else [VMEM(shape, bf16), *scratch],
        compiler_params=pltpu.CompilerParams(vmem_limit_bytes=24 * 2**20),
    )(codes, place, x, weights, ends, near, far)


def dot_rows(planes, matrix):
    rows = planes.shape[0] * planes.shape[1]
    return jnp.dot(planes.reshape(rows, planes.shape[2]), matrix, preferred_element_type=f32)


def forward_kernel(codes, place, x_ref, dy_ref, w_ref, gain_ref, conv_ref, middle_ref, *refs):
    halo, refs = refs[:4], refs[4:]
    out_ref, pre_grad_ref, scaled_ref, keep_ref, send_ref, far_ref = refs[:6]
    table, planes, rim_planes, conv_all, shifted, shifted_rim, staged, sems = refs[6:]
    fill_table(place, table, x_ref[...], halo)
    unfold(codes, table, planes, rim_planes, RIM)
    conv_all[...] = conv_ref[...]
    conv_all[:, :64] += dot_rows(rim_planes[:, 0], w_ref[0]).reshape(CAP, 64, C)
    conv_all[:, 448:] += dot_rows(rim_planes[:, 1], w_ref[2]).reshape(CAP, 64, C)
    gain = gain_ref[...]
    gain_sum = jnp.zeros((1, C), f32)
    for s in range(CAP):
        conv = conv_all[s]
        occupied = codes[s, 13] >= 0
        upstream = jnp.where(occupied, dy_ref[s].astype(f32), 0.0)
        pre_act = jnp.where(occupied, x_ref[s].astype(f32), 0.0) + gain * conv
        sig = jax.nn.sigmoid(pre_act)
        staged[s] = (pre_act * sig).astype(bf16)
        pltpu.make_async_copy(staged.at[s], out_ref.at[s], sems.at[s]).start()
        pre_grad = upstream * sig * (1.0 + pre_act * (1.0 - sig))
        pre_grad_ref[s] = pre_grad
        scaled = (gain * pre_grad).astype(bf16)
        scaled_ref[s] = scaled
        gain_sum = gain_sum + jnp.sum(pre_grad * conv, axis=0, keepdims=True)
        scaled = scaled.reshape(8, 64, C)
        zero = jnp.zeros((64, C), bf16)
        shifted[s, :7, :, :C] = scaled[1:]
        shifted[s, 7, :, :C] = zero
        shifted[s, :, :, C : 2 * C] = scaled
        shifted[s, 0, :, 2 * C :] = zero
        shifted[s, 1:, :, 2 * C :] = scaled[:7]
        shifted_rim[s] = jnp.zeros((2, 64, 3 * C), bf16)
        shifted_rim[s, 0, :, :C] = scaled[0]
        shifted_rim[s, 1, :, 2 * C :] = scaled[7]
    core = place[CORE]
    low, high = y_planes(scaled_ref[...])
    far_ref[...] = jnp.where(core == 0, low, high).astype(bf16)
    send_ref[HALF * C :] = jnp.where(core == 0, high, low).astype(bf16)
    for own in (0, 1):
        pl.when(core == own)(
            lambda own=own: weight_terms(
                own, gain_sum, ((middle_ref, shifted, CAP * 512), (rim_planes, shifted_rim, CAP * 128)), keep_ref, send_ref
            )
        )
    for s in range(CAP):
        pltpu.make_async_copy(staged.at[s], out_ref.at[s], sems.at[s]).wait()


def weight_terms(own, gain_sum, pairs, keep_ref, send_ref):
    def put(half, at, value):
        ref = keep_ref if half == own else send_ref
        ref[at : at + value.shape[0]] = value.astype(ref.dtype)

    for bc in range(9):
        term = jnp.zeros((C, 3 * C), f32)
        for source, target, rows in pairs:
            lhs = source[:, :, :, C * bc : C * bc + C].reshape(rows, C)
            rhs = target[...].reshape(rows, 3 * C)
            term = term + lax.dot_general(lhs, rhs, (((0,), (0,)), ((), ())), preferred_element_type=f32)
        for a in range(3):
            half, block = divmod(9 * a + bc, HALF)
            put(half, C * block, term[:, C * a : C * a + C])
    first = jnp.concatenate([gain_sum, jnp.zeros((7, C), f32)], axis=0)
    high = first.astype(bf16).astype(f32)
    rows = [jnp.zeros((GAIN_ROW, C), f32), high, first - high, jnp.zeros((C - GAIN_ROW - 16, C), f32)]
    put(1, C * (HALF - 1), jnp.concatenate(rows, axis=0))


def forward(codes, place, x, dy, weights, gain, conv, unfolded, halo):
    vmem = pl.BlockSpec(memory_space=VMEM)
    smem = pl.BlockSpec(memory_space=pltpu.SMEM)
    return pl.pallas_call(
        forward_kernel,
        out_shape=[
            BLOCK,
            jax.ShapeDtypeStruct((CAP, 512, C), f32),
            BLOCK,
            jax.ShapeDtypeStruct((HALF * C, C), f32),
            jax.ShapeDtypeStruct((HALF * C + CAP * 64, C), bf16),
            jax.ShapeDtypeStruct((CAP * 64, C), bf16),
        ],
        in_specs=[smem] * 2 + [vmem] * 10,
        out_specs=[pl.BlockSpec(memory_space=pltpu.HBM)] + [vmem] * 5,
        scratch_shapes=[
            VMEM((EMPTY + 1, 8, 64, C), f32),
            VMEM((3, 2, 80, C), f32),
            VMEM((CAP, 2, 64, 9 * C), bf16),
            VMEM((CAP, 512, C), f32),
            VMEM((CAP, 8, 64, 3 * C), bf16),
            VMEM((CAP, 2, 64, 3 * C), bf16),
            VMEM((CAP, 512, C), bf16),
            pltpu.SemaphoreType.DMA((CAP,)),
        ],
        compiler_params=pltpu.CompilerParams(vmem_limit_bytes=32 * 2**20),
    )(codes, place, x, dy, weights, gain, conv, unfolded, *halo)


def backward_kernel(codes, place, scaled_ref, w_ref, pre_grad_ref, conv_ref, *refs):
    halo, (grad_ref, table, planes, rim_planes, staged, total, sems) = refs[:4], refs[4:]
    fill_table(place, table, scaled_ref[...], halo)
    unfold(codes, table, planes, rim_planes, RIM)
    total[...] = pre_grad_ref[...] + conv_ref[...]
    total[:, :64] += dot_rows(rim_planes[:, 0], w_ref[0]).reshape(CAP, 64, C)
    total[:, 448:] += dot_rows(rim_planes[:, 1], w_ref[2]).reshape(CAP, 64, C)
    staged[...] = total[...].astype(bf16)
    copy = pltpu.make_async_copy(staged, grad_ref, sems)
    copy.start()
    copy.wait()


def backward(codes, place, scaled, weights, pre_grad, conv, halo):
    vmem = pl.BlockSpec(memory_space=VMEM)
    return pl.pallas_call(
        backward_kernel,
        out_shape=BLOCK,
        in_specs=[pl.BlockSpec(memory_space=pltpu.SMEM)] * 2 + [vmem] * 8,
        out_specs=pl.BlockSpec(memory_space=pltpu.HBM),
        scratch_shapes=[
            VMEM((EMPTY + 1, 8, 64, C), f32),
            VMEM((3, 2, 80, C), f32),
            VMEM((CAP, 2, 64, 9 * C), bf16),
            VMEM((CAP, 512, C), bf16),
            VMEM((CAP, 512, C), f32),
            pltpu.SemaphoreType.DMA,
        ],
        compiler_params=pltpu.CompilerParams(vmem_limit_bytes=32 * 2**20),
    )(codes, place, scaled, weights, pre_grad, conv, *halo)


def pair_kernel(place, keep_ref, arrived_ref, out_hbm, near_ref, staged, sems):
    near_ref[...] = arrived_ref[HALF * C :]
    chunks, rows, _ = staged.shape
    copies = []
    for i in range(0, chunks, chunks // PIECES):
        piece = slice(i, i + chunks // PIECES)
        flat = slice(i * rows, (i + chunks // PIECES) * rows)
        total = keep_ref[flat] + arrived_ref[flat].astype(f32)
        at = (HALF - 1) * C + GAIN_ROW - flat.start
        if flat.stop == HALF * C:
            total = split_gain(total, at, place[CORE] == 1)
        staged[piece] = total.astype(bf16).reshape(chunks // PIECES, rows, C)
        copies.append(pltpu.make_async_copy(staged.at[piece], out_hbm.at[piece], sems.at[len(copies)]))
        copies[-1].start()
    for copy in copies:
        copy.wait()


def pair_sum(place, keep, arrived, chunks):
    smem, vmem, hbm = (pl.BlockSpec(memory_space=m) for m in (pltpu.SMEM, VMEM, pltpu.HBM))
    shape = (chunks, HALF * C // chunks, C)
    return pl.pallas_call(
        pair_kernel,
        out_shape=[jax.ShapeDtypeStruct(shape, bf16), jax.ShapeDtypeStruct((CAP * 64, C), bf16)],
        in_specs=[smem, vmem, vmem],
        out_specs=[hbm, vmem],
        scratch_shapes=[VMEM(shape, bf16), pltpu.SemaphoreType.DMA((PIECES,))],
        compiler_params=pltpu.CompilerParams(vmem_limit_bytes=8 * 2**20),
    )(place, keep, arrived)


def sum_kernel(place, parts_ref, out_ref):
    total = jnp.sum(parts_ref[...].astype(f32), axis=0)
    total = split_gain(total, total.shape[0] - C + GAIN_ROW, place[LAST] == 1)
    out_ref[...] = jnp.broadcast_to(total.astype(bf16)[None], out_ref.shape)


def sum_of(place, parts, count):
    return small(sum_kernel, jax.ShapeDtypeStruct((count, *parts.shape[1:]), bf16), 8, place, parts)


def finish_kernel(place, mine_ref, other_ref, weight_hbm, gain_hbm, staged, sems, gain_ref, gain_sem):
    at = (HALF - 1) * C + GAIN_ROW
    gain_copy = pltpu.make_async_copy(gain_ref, gain_hbm, gain_sem)
    pieces = ((0, 0, 7), (0, 7, 14), (1, 0, 7), (1, 7, 13))
    copies = []
    for i, (half, start, stop) in enumerate(pieces):
        here = slice(HALF * half + start, HALF * half + stop)
        copies.append(pltpu.make_async_copy(staged.at[here], weight_hbm.at[here], sems.at[i]))

    def write(halves):
        pair = halves[1][...].reshape(HALF * C, C)[at : at + 16].astype(f32)
        gain_ref[...] = pair[:1] + pair[8:9]
        gain_copy.start()
        for copy, (half, start, stop) in zip(copies, pieces):
            rows = halves[half][...].reshape(HALF, C, C)[start:stop]
            staged[HALF * half + start : HALF * half + stop] = rows.astype(f32)
            copy.start()

    pl.when(place[CORE] == 0)(lambda: write((mine_ref, other_ref)))
    pl.when(place[CORE] == 1)(lambda: write((other_ref, mine_ref)))
    gain_copy.wait()
    for copy in copies:
        copy.wait()


def finish(place, mine, other):
    smem, vmem, hbm = (pl.BlockSpec(memory_space=m) for m in (pltpu.SMEM, VMEM, pltpu.HBM))
    return pl.pallas_call(
        finish_kernel,
        out_shape=[jax.ShapeDtypeStruct((27, C, C), f32), jax.ShapeDtypeStruct((1, C), f32)],
        in_specs=[smem, vmem, vmem],
        out_specs=[hbm, hbm],
        scratch_shapes=[
            VMEM((27, C, C), f32),
            pltpu.SemaphoreType.DMA((4,)),
            VMEM((1, C), f32),
            pltpu.SemaphoreType.DMA,
        ],
        compiler_params=pltpu.CompilerParams(vmem_limit_bytes=8 * 2**20),
    )(place, mine, other)


def small(kernel, out_shape, megabytes, scalars, *operands):
    vmem = pl.BlockSpec(memory_space=VMEM)
    smem = [] if scalars is None else [scalars]
    return pl.pallas_call(
        kernel,
        out_shape=out_shape,
        in_specs=[pl.BlockSpec(memory_space=pltpu.SMEM)] * len(smem) + [vmem] * len(operands),
        out_specs=jax.tree.map(lambda _: vmem, out_shape),
        compiler_params=pltpu.CompilerParams(vmem_limit_bytes=megabytes * 2**20),
    )(*smem, *operands)


def trade(parts, axes):
    return lax.all_to_all(parts, axes, 0, 0, tiled=True)


def on_device(features, cotangent, neighbours, weights, channel_gain):
    together = lax.optimization_barrier
    plane, line = ("y", "x"), ("zl", "zh")
    n_plane, n_line = lax.axis_size(plane), lax.axis_size(line)
    core = lax.axis_index("core")
    last = core * (lax.axis_index(plane) == n_plane - 1)
    place = jnp.stack([core, lax.axis_index("x") % 2, last]).astype(jnp.int32)
    near, far, x = rims_of(place, features[0, 0])
    near, far, (matrices, codes, adjoint, ends, adjoint_ends) = together(
        (swap_core(near), swap_far(far), prepare(weights, neighbours[0, 0]))
    )
    first, second = widen(place, near, far, x)
    conv, unfolded = middle(codes, place, x, matrices, ends, near, far, True)
    first, second, dy, conv, unfolded = together(
        (swap_x(first, 0), swap_x(second, 1), fetch(cotangent[0, 0]), conv, unfolded)
    )
    halo = (near, far, first, second)
    result, pre_grad, scaled, keep, send, far = forward(
        codes, place, x, dy, matrices, channel_gain.reshape(1, C), conv, unfolded, halo
    )

    parts, near = pair_sum(place, keep, swap_core(send), n_plane)
    far, parts = together((swap_far(far), trade(parts, plane)))
    first, second = widen(place, near, far, scaled)
    parts = sum_of(place, parts, n_line)
    (conv,) = middle(codes, place, scaled, adjoint, adjoint_ends, near, far, False)
    first, conv, parts = together((swap_x(first, 0), conv, trade(parts, line)))
    parts = sum_of(place, parts, n_plane)
    second, mine = together((swap_x(second, 1), trade(parts, plane)))
    grad = backward(codes, place, scaled, adjoint, pre_grad, conv, (near, far, first, second))
    grad, other = together((grad, swap_core(mine)))
    weight_grad, gain_grad = finish(place, mine, other)
    return (result[None, None], grad[None, None], weight_grad, gain_grad.reshape(C))


def solution(mesh):
    physical = Mesh(mesh.devices.reshape(SPLIT), AXES)
    gx, gy = ("y", "zl", "x"), ("zh", "core")
    split = P(gx, gy, None, None, None)
    return jax.shard_map(
        on_device,
        mesh=physical,
        in_specs=(split, split, P(gx, gy, None, None), P(), P()),
        out_specs=(split, split, P(), P()),
        check_vma=False,
    )
```

```python
import jax
import jax.numpy as jnp
from jax import lax
from jax.experimental import pallas as pl
from jax.experimental.pallas import tpu as pltpu
from jax.sharding import Mesh, PartitionSpec as P

C = 128
CAP = 2
SIDE = (-1, 0, 1)
EMPTY = 9 * CAP
HALF = 14
GAIN_ROW = 16
PIECES = 2
CORE, ODD, LAST = 0, 1, 2
SPLIT = (4, 2, 4, 4, 2)
AXES = ("y", "zl", "x", "zh", "core")
VMEM = pltpu.VMEM
f32 = jnp.float32
bf16 = jnp.bfloat16
BLOCK = jax.ShapeDtypeStruct((CAP, 512, C), bf16)


def rim(d):
    return {-1: (7, 1), 0: (0, 8), 1: (0, 1)}[d]


def span(d):
    return {-1: (0, 1), 0: (1, 8), 1: (9, 1)}[d]


def position():
    core = lax.axis_index("core")
    x, y = lax.axis_index("x"), lax.axis_index("y")
    is_last = (x == lax.axis_size("x") - 1) & (y == lax.axis_size("y") - 1) & (core == 1)
    return core, lax.rem(x, 2), is_last.astype(jnp.int32)


def y_planes(value):
    value = value.astype(f32).reshape(CAP, 8, 8, 8, C)
    return [value[:, :, y].reshape(CAP * 64, C) for y in (0, 7)]


def rims_kernel(x_ref, near_ref, far_ref, x_out):
    place = position()
    x_out[...] = x_ref[...]
    low, high = y_planes(x_ref[...])
    first = place[CORE] == 0
    near_ref[...] = jnp.where(first, high, low).astype(bf16)
    far_ref[...] = jnp.where(first, low, high).astype(bf16)


def rims_of(x):
    plane = jax.ShapeDtypeStruct((CAP * 64, C), bf16)
    return small(rims_kernel, [plane, plane, BLOCK], 8, None, x)


def prepare_kernel(w_ref, codes_ref, w_out, codes_out, adjoint_ref, ends_ref, adjoint_ends_ref):
    codes_out[...] = codes_ref[...]
    for k in range(27):
        a, at = k // 9, C * (k % 9)
        w_out[a, at : at + C] = w_ref[k]
        matrix = w_ref[26 - k].astype(f32).T.astype(bf16)
        adjoint_ref[a, at : at + C] = matrix
        if a != 1:
            column = 0 if a == 0 else C
            adjoint_ends_ref[at : at + C, column : column + C] = matrix
            ends_ref[at : at + C, column : column + C] = w_ref[k]


def prepare(weights, codes):
    ends = jax.ShapeDtypeStruct((9 * C, 2 * C), bf16)
    matrices = jax.ShapeDtypeStruct((3, 9 * C, C), bf16)
    shapes = [matrices, jax.ShapeDtypeStruct(codes.shape, codes.dtype), matrices, ends, ends]
    return small(prepare_kernel, shapes, 8, None, weights, codes)


def fetch_kernel(value_ref, out_ref):
    out_ref[...] = value_ref[...]


def fetch(value):
    return small(fetch_kernel, BLOCK, 8, None, value)


def widen_kernel(near_ref, far_ref, x_ref, first_ref, second_ref):
    place = position()
    before, after = sides(place[CORE] == 0, near_ref, far_ref)
    wide = []
    for x in (0, 7):
        middle = x_ref[:, 64 * x : 64 * x + 64].astype(f32).reshape(CAP, 8, 8, C)
        ends = [v.reshape(CAP, 8, 8, C)[:, x : x + 1] for v in (before, after)]
        wide.append(jnp.concatenate([ends[0], middle, ends[1]], axis=1).reshape(CAP * 80, C))
    even = place[ODD] == 0
    first_ref[...] = jnp.where(even, wide[1], wide[0]).astype(bf16)
    second_ref[...] = jnp.where(even, wide[0], wide[1]).astype(bf16)


def widen(near, far, x):
    shapes = [jax.ShapeDtypeStruct((CAP * 80, C), bf16)] * 2
    return small(widen_kernel, shapes, 8, None, near, far, x)


def sides(first, one_ref, other_ref):
    one, other = one_ref[...].astype(f32), other_ref[...].astype(f32)
    return jnp.where(first, other, one), jnp.where(first, one, other)


def swap_far(value):
    n = lax.axis_size("zh")
    pairs = [(2 * i + 1, 2 * i + 2) for i in range(n - 1)]
    return lax.ppermute(value, ("zh", "core"), pairs + [(b, a) for a, b in pairs])


def swap_x(value, odd):
    axes = ("y", "zl", "x")
    pairs = [(i, i + 1) for i in range(odd, lax.axis_size(axes) - 1, 2)]
    return lax.ppermute(value, axes, pairs + [(b, a) for a, b in pairs])


def swap_core(value):
    return lax.ppermute(value, "core", [(0, 1), (1, 0)])


def fill_own(place, table, own, near, far, planes):
    own = own.astype(f32).reshape(CAP, 8, 64, C)
    for x in planes:
        table[4 * CAP : 5 * CAP, x] = own[:, x]
        table[EMPTY, x] = jnp.zeros((64, C), f32)
    for value, device, y in zip(sides(place[CORE] == 0, near, far), (3, 5), (7, 0)):
        table[device * CAP : (device + 1) * CAP, :, 8 * y : 8 * y + 8] = value.reshape(CAP, 8, 8, C)


def fill_table(place, table, own, halo):
    near, far, first, second = halo
    fill_own(place, table, own, near, far, (0, 7))
    for value, dx, x in zip(sides(place[ODD] == 0, first, second), (0, 2), (7, 0)):
        wide = value.reshape(CAP, 80, C)
        for dy, at, y, count in ((0, 0, 7, 1), (1, 1, 0, 8), (2, 9, 0, 1)):
            device = 3 * dx + dy
            table[device * CAP : (device + 1) * CAP, x, 8 * y : 8 * (y + count)] = wide[:, 8 * at : 8 * (at + count)]


ALL = {-1: 0, 0: 1, 1: 9}
MIDDLE = {0: 0}
RIM = {-1: 0, 1: 1}


def unfold(codes, table, planes, unfolded, places):
    height = lax.broadcasted_iota(jnp.int32, (1, 8, C), 1)
    for s in range(CAP):
        for a, xd in places.items():
            for b in SIDE:
                (xs, nx), (ys, ny) = rim(a), rim(b)
                yd, _ = span(b)
                parts = []
                for c in SIDE:
                    code = codes[s, 9 * (a + 1) + 3 * (b + 1) + (c + 1)]
                    code = jnp.where(code < 0, EMPTY, code)
                    part = table[code, xs : xs + nx, 8 * ys : 8 * (ys + ny), :]
                    parts.append(part.reshape(nx * ny, 8, C))
                below, here, above = parts
                down = pltpu.roll(jnp.where(height == 7, below, here), 1, 1)
                up = pltpu.roll(jnp.where(height == 0, above, here), 7, 1)
                for i, part in enumerate((down, here, up)):
                    planes[i, xd : xd + nx, 8 * yd : 8 * (yd + ny), :] = part.reshape(nx, ny * 8, C)
        for b in SIDE:
            for c in SIDE:
                at = C * (3 * (b + 1) + (c + 1))
                unfolded[s, :, :, at : at + C] = planes[c + 1, :, 8 * (1 + b) : 8 * (1 + b) + 64, :].astype(bf16)


def split_gain(rows, at, here):
    total = rows[at : at + 8] + rows[at + 8 : at + 16]
    high = total.astype(bf16).astype(f32)
    pair = jnp.concatenate([high, total - high], axis=0)
    pair = jnp.where(here, pair, rows[at : at + 16])
    pieces = [rows[:at]] if at else []
    return jnp.concatenate([*pieces, pair, rows[at + 16 :]], axis=0)


def middle_kernel(codes, x_ref, w_ref, ends_ref, near_ref, far_ref, conv_ref, middle_ref, table, planes):
    place = position()
    fill_own(place, table, x_ref[...], near_ref, far_ref, range(8))
    unfold(codes, table, planes, middle_ref, MIDDLE)
    for s in range(CAP):
        ends = dot_rows(middle_ref[s], ends_ref[...])
        conv_ref[s] = dot_rows(middle_ref[s], w_ref[1])
        conv_ref[s, 64:] += ends[:448, :C]
        conv_ref[s, :448] += ends[64:, C:]


def middle(codes, x, weights, ends, near, far, keep):
    vmem = pl.BlockSpec(memory_space=VMEM)
    smem = pl.BlockSpec(memory_space=pltpu.SMEM)
    conv = jax.ShapeDtypeStruct((CAP, 512, C), f32)
    scratch = [VMEM((EMPTY + 1, 8, 64, C), f32), VMEM((3, 8, 80, C), f32)]
    shape = (CAP, 8, 64, 9 * C)
    return pl.pallas_call(
        middle_kernel,
        out_shape=[conv, jax.ShapeDtypeStruct(shape, bf16)] if keep else [conv],
        in_specs=[smem] + [vmem] * 5,
        out_specs=[vmem] * (2 if keep else 1),
        scratch_shapes=scratch if keep else [VMEM(shape, bf16), *scratch],
        compiler_params=pltpu.CompilerParams(vmem_limit_bytes=24 * 2**20),
    )(codes, x, weights, ends, near, far)


def dot_rows(planes, matrix):
    rows = planes.shape[0] * planes.shape[1]
    return jnp.dot(planes.reshape(rows, planes.shape[2]), matrix, preferred_element_type=f32)


def forward_kernel(codes, x_ref, dy_ref, w_ref, gain_ref, conv_ref, middle_ref, *refs):
    place = position()
    halo, refs = refs[:4], refs[4:]
    out_ref, pre_grad_ref, scaled_ref, keep_ref, send_ref, far_ref = refs[:6]
    table, planes, rim_planes, conv_all, shifted, shifted_rim, staged, sems = refs[6:]
    fill_table(place, table, x_ref[...], halo)
    unfold(codes, table, planes, rim_planes, RIM)
    conv_all[...] = conv_ref[...]
    conv_all[:, :64] += dot_rows(rim_planes[:, 0], w_ref[0]).reshape(CAP, 64, C)
    conv_all[:, 448:] += dot_rows(rim_planes[:, 1], w_ref[2]).reshape(CAP, 64, C)
    gain = gain_ref[...]
    gain_sum = jnp.zeros((1, C), f32)
    for s in range(CAP):
        conv = conv_all[s]
        occupied = codes[s, 13] >= 0
        upstream = jnp.where(occupied, dy_ref[s].astype(f32), 0.0)
        pre_act = jnp.where(occupied, x_ref[s].astype(f32), 0.0) + gain * conv
        sig = jax.nn.sigmoid(pre_act)
        staged[s] = (pre_act * sig).astype(bf16)
        pltpu.make_async_copy(staged.at[s], out_ref.at[s], sems.at[s]).start()
        pre_grad = upstream * sig * (1.0 + pre_act * (1.0 - sig))
        pre_grad_ref[s] = pre_grad
        scaled = (gain * pre_grad).astype(bf16)
        scaled_ref[s] = scaled
        gain_sum = gain_sum + jnp.sum(pre_grad * conv, axis=0, keepdims=True)
        scaled = scaled.reshape(8, 64, C)
        zero = jnp.zeros((64, C), bf16)
        shifted[s, :7, :, :C] = scaled[1:]
        shifted[s, 7, :, :C] = zero
        shifted[s, :, :, C : 2 * C] = scaled
        shifted[s, 0, :, 2 * C :] = zero
        shifted[s, 1:, :, 2 * C :] = scaled[:7]
        shifted_rim[s] = jnp.zeros((2, 64, 3 * C), bf16)
        shifted_rim[s, 0, :, :C] = scaled[0]
        shifted_rim[s, 1, :, 2 * C :] = scaled[7]
    core = place[CORE]
    low, high = y_planes(scaled_ref[...])
    far_ref[...] = jnp.where(core == 0, low, high).astype(bf16)
    send_ref[HALF * C :] = jnp.where(core == 0, high, low).astype(bf16)
    for own in (0, 1):
        pl.when(core == own)(
            lambda own=own: weight_terms(
                own, gain_sum, ((middle_ref, shifted, CAP * 512), (rim_planes, shifted_rim, CAP * 128)), keep_ref, send_ref
            )
        )
    for s in range(CAP):
        pltpu.make_async_copy(staged.at[s], out_ref.at[s], sems.at[s]).wait()


def weight_terms(own, gain_sum, pairs, keep_ref, send_ref):
    def put(half, at, value):
        ref = keep_ref if half == own else send_ref
        ref[at : at + value.shape[0]] = value.astype(ref.dtype)

    for bc in range(9):
        term = jnp.zeros((C, 3 * C), f32)
        for source, target, rows in pairs:
            lhs = source[:, :, :, C * bc : C * bc + C].reshape(rows, C)
            rhs = target[...].reshape(rows, 3 * C)
            term = term + lax.dot_general(lhs, rhs, (((0,), (0,)), ((), ())), preferred_element_type=f32)
        for a in range(3):
            half, block = divmod(9 * a + bc, HALF)
            put(half, C * block, term[:, C * a : C * a + C])
    first = jnp.concatenate([gain_sum, jnp.zeros((7, C), f32)], axis=0)
    high = first.astype(bf16).astype(f32)
    rows = [jnp.zeros((GAIN_ROW, C), f32), high, first - high, jnp.zeros((C - GAIN_ROW - 16, C), f32)]
    put(1, C * (HALF - 1), jnp.concatenate(rows, axis=0))


def forward(codes, x, dy, weights, gain, conv, unfolded, halo):
    vmem = pl.BlockSpec(memory_space=VMEM)
    smem = pl.BlockSpec(memory_space=pltpu.SMEM)
    return pl.pallas_call(
        forward_kernel,
        out_shape=[
            BLOCK,
            jax.ShapeDtypeStruct((CAP, 512, C), f32),
            BLOCK,
            jax.ShapeDtypeStruct((HALF * C, C), f32),
            jax.ShapeDtypeStruct((HALF * C + CAP * 64, C), bf16),
            jax.ShapeDtypeStruct((CAP * 64, C), bf16),
        ],
        in_specs=[smem] + [vmem] * 10,
        out_specs=[pl.BlockSpec(memory_space=pltpu.HBM)] + [vmem] * 5,
        scratch_shapes=[
            VMEM((EMPTY + 1, 8, 64, C), f32),
            VMEM((3, 2, 80, C), f32),
            VMEM((CAP, 2, 64, 9 * C), bf16),
            VMEM((CAP, 512, C), f32),
            VMEM((CAP, 8, 64, 3 * C), bf16),
            VMEM((CAP, 2, 64, 3 * C), bf16),
            VMEM((CAP, 512, C), bf16),
            pltpu.SemaphoreType.DMA((CAP,)),
        ],
        compiler_params=pltpu.CompilerParams(vmem_limit_bytes=32 * 2**20),
    )(codes, x, dy, weights, gain, conv, unfolded, *halo)


def backward_kernel(codes, scaled_ref, w_ref, pre_grad_ref, conv_ref, *refs):
    place = position()
    halo, (grad_ref, table, planes, rim_planes, staged, total, sems) = refs[:4], refs[4:]
    fill_table(place, table, scaled_ref[...], halo)
    unfold(codes, table, planes, rim_planes, RIM)
    total[...] = pre_grad_ref[...] + conv_ref[...]
    total[:, :64] += dot_rows(rim_planes[:, 0], w_ref[0]).reshape(CAP, 64, C)
    total[:, 448:] += dot_rows(rim_planes[:, 1], w_ref[2]).reshape(CAP, 64, C)
    staged[...] = total[...].astype(bf16)
    copy = pltpu.make_async_copy(staged, grad_ref, sems)
    copy.start()
    copy.wait()


def backward(codes, scaled, weights, pre_grad, conv, halo):
    vmem = pl.BlockSpec(memory_space=VMEM)
    return pl.pallas_call(
        backward_kernel,
        out_shape=BLOCK,
        in_specs=[pl.BlockSpec(memory_space=pltpu.SMEM)] + [vmem] * 8,
        out_specs=pl.BlockSpec(memory_space=pltpu.HBM),
        scratch_shapes=[
            VMEM((EMPTY + 1, 8, 64, C), f32),
            VMEM((3, 2, 80, C), f32),
            VMEM((CAP, 2, 64, 9 * C), bf16),
            VMEM((CAP, 512, C), bf16),
            VMEM((CAP, 512, C), f32),
            pltpu.SemaphoreType.DMA,
        ],
        compiler_params=pltpu.CompilerParams(vmem_limit_bytes=32 * 2**20),
    )(codes, scaled, weights, pre_grad, conv, *halo)


def pair_kernel(keep_ref, arrived_ref, out_hbm, near_ref, staged, sems):
    place = position()
    near_ref[...] = arrived_ref[HALF * C :]
    chunks, rows, _ = staged.shape
    copies = []
    for i in range(0, chunks, chunks // PIECES):
        piece = slice(i, i + chunks // PIECES)
        flat = slice(i * rows, (i + chunks // PIECES) * rows)
        total = keep_ref[flat] + arrived_ref[flat].astype(f32)
        at = (HALF - 1) * C + GAIN_ROW - flat.start
        if flat.stop == HALF * C:
            total = split_gain(total, at, place[CORE] == 1)
        staged[piece] = total.astype(bf16).reshape(chunks // PIECES, rows, C)
        copies.append(pltpu.make_async_copy(staged.at[piece], out_hbm.at[piece], sems.at[len(copies)]))
        copies[-1].start()
    for copy in copies:
        copy.wait()


def pair_sum(keep, arrived, chunks):
    smem, vmem, hbm = (pl.BlockSpec(memory_space=m) for m in (pltpu.SMEM, VMEM, pltpu.HBM))
    shape = (chunks, HALF * C // chunks, C)
    return pl.pallas_call(
        pair_kernel,
        out_shape=[jax.ShapeDtypeStruct(shape, bf16), jax.ShapeDtypeStruct((CAP * 64, C), bf16)],
        in_specs=[vmem, vmem],
        out_specs=[hbm, vmem],
        scratch_shapes=[VMEM(shape, bf16), pltpu.SemaphoreType.DMA((PIECES,))],
        compiler_params=pltpu.CompilerParams(vmem_limit_bytes=8 * 2**20),
    )(keep, arrived)


def sum_kernel(parts_ref, out_ref):
    place = position()
    total = jnp.sum(parts_ref[...].astype(f32), axis=0)
    total = split_gain(total, total.shape[0] - C + GAIN_ROW, place[LAST] == 1)
    out_ref[...] = jnp.broadcast_to(total.astype(bf16)[None], out_ref.shape)


def sum_of(parts, count):
    return small(sum_kernel, jax.ShapeDtypeStruct((count, *parts.shape[1:]), bf16), 8, None, parts)


def finish_kernel(mine_ref, other_ref, weight_hbm, gain_hbm, staged, sems, gain_ref, gain_sem):
    place = position()
    at = (HALF - 1) * C + GAIN_ROW
    gain_copy = pltpu.make_async_copy(gain_ref, gain_hbm, gain_sem)
    pieces = ((0, 0, 7), (0, 7, 14), (1, 0, 7), (1, 7, 13))
    copies = []
    for i, (half, start, stop) in enumerate(pieces):
        here = slice(HALF * half + start, HALF * half + stop)
        copies.append(pltpu.make_async_copy(staged.at[here], weight_hbm.at[here], sems.at[i]))

    def write(halves):
        pair = halves[1][...].reshape(HALF * C, C)[at : at + 16].astype(f32)
        gain_ref[...] = pair[:1] + pair[8:9]
        gain_copy.start()
        for copy, (half, start, stop) in zip(copies, pieces):
            rows = halves[half][...].reshape(HALF, C, C)[start:stop]
            staged[HALF * half + start : HALF * half + stop] = rows.astype(f32)
            copy.start()

    pl.when(place[CORE] == 0)(lambda: write((mine_ref, other_ref)))
    pl.when(place[CORE] == 1)(lambda: write((other_ref, mine_ref)))
    gain_copy.wait()
    for copy in copies:
        copy.wait()


def finish(mine, other):
    smem, vmem, hbm = (pl.BlockSpec(memory_space=m) for m in (pltpu.SMEM, VMEM, pltpu.HBM))
    return pl.pallas_call(
        finish_kernel,
        out_shape=[jax.ShapeDtypeStruct((27, C, C), f32), jax.ShapeDtypeStruct((1, C), f32)],
        in_specs=[vmem, vmem],
        out_specs=[hbm, hbm],
        scratch_shapes=[
            VMEM((27, C, C), f32),
            pltpu.SemaphoreType.DMA((4,)),
            VMEM((1, C), f32),
            pltpu.SemaphoreType.DMA,
        ],
        compiler_params=pltpu.CompilerParams(vmem_limit_bytes=8 * 2**20),
    )(mine, other)


def small(kernel, out_shape, megabytes, scalars, *operands):
    vmem = pl.BlockSpec(memory_space=VMEM)
    smem = [] if scalars is None else [scalars]
    return pl.pallas_call(
        kernel,
        out_shape=out_shape,
        in_specs=[pl.BlockSpec(memory_space=pltpu.SMEM)] * len(smem) + [vmem] * len(operands),
        out_specs=jax.tree.map(lambda _: vmem, out_shape),
        compiler_params=pltpu.CompilerParams(vmem_limit_bytes=megabytes * 2**20),
    )(*smem, *operands)


def trade(parts, axes):
    return lax.all_to_all(parts, axes, 0, 0, tiled=True)


def on_device(features, cotangent, neighbours, weights, channel_gain):
    together = lax.optimization_barrier
    plane, line = ("y", "x"), ("zl", "zh")
    n_plane, n_line = lax.axis_size(plane), lax.axis_size(line)
    near, far, x = rims_of(features[0, 0])
    near, far, (matrices, codes, adjoint, ends, adjoint_ends) = together(
        (swap_core(near), swap_far(far), prepare(weights, neighbours[0, 0]))
    )
    first, second = widen(near, far, x)
    conv, unfolded = middle(codes, x, matrices, ends, near, far, True)
    first, second, dy, conv, unfolded = together(
        (swap_x(first, 0), swap_x(second, 1), fetch(cotangent[0, 0]), conv, unfolded)
    )
    halo = (near, far, first, second)
    result, pre_grad, scaled, keep, send, far = forward(
        codes, x, dy, matrices, channel_gain.reshape(1, C), conv, unfolded, halo
    )

    parts, near = pair_sum(keep, swap_core(send), n_plane)
    far, parts = together((swap_far(far), trade(parts, plane)))
    first, second = widen(near, far, scaled)
    parts = sum_of(parts, n_line)
    (conv,) = middle(codes, scaled, adjoint, adjoint_ends, near, far, False)
    first, conv, parts = together((swap_x(first, 0), conv, trade(parts, line)))
    parts = sum_of(parts, n_plane)
    second, mine = together((swap_x(second, 1), trade(parts, plane)))
    grad = backward(codes, scaled, adjoint, pre_grad, conv, (near, far, first, second))
    grad, other = together((grad, swap_core(mine)))
    weight_grad, gain_grad = finish(mine, other)
    return (result[None, None], grad[None, None], weight_grad, gain_grad.reshape(C))


def solution(mesh):
    physical = Mesh(mesh.devices.reshape(SPLIT), AXES)
    gx, gy = ("y", "zl", "x"), ("zh", "core")
    split = P(gx, gy, None, None, None)
    return jax.shard_map(
        on_device,
        mesh=physical,
        in_specs=(split, split, P(gx, gy, None, None), P(), P()),
        out_specs=(split, split, P(), P()),
        check_vma=False,
    )
```
